256 devices in a mesh: dp: 2 (over z_lo), mx: 16 (over x, z_hi), my: 8 (over y, core).
Axes of the slice: x: 4, y: 4, z: 8 (z_hi: 4, z_lo: 2; z = z_hi * 2 + z_lo), core: 2. Of those that a mesh axis runs over, the one named last changes fastest.
Arguments:
- crops_in: bfloat16 [16, 257, 6144], P(('dp', 'my')), may hold values from -24 to 24
- crop_table: int32 [16], replicated, may hold values from 0 to 15, each once
- ln_gain: bfloat16 [6144], P('my'), may hold values from 0.099609375 to 1.8984375
- w_qkv: bfloat16 [6144, 48, 3, 128], P('my', 'mx'), may hold values from -0.078125 to 0.078125
- q_gain: float32 [48, 128], P('mx'), may hold values from 0.5 to 7
- k_gain: float32 [48, 128], P('mx'), may hold values from 0.5 to 7
- w_up: bfloat16 [6144, 24576], P('my', 'mx'), may hold values from -0.078125 to 0.078125
- b_up: float32 [24576], P('mx'), may hold values from -3 to 3
- w_out: bfloat16 [48, 128, 6144], P('mx', None, 'my'), may hold values from -0.078125 to 0.078125
- w_down: bfloat16 [24576, 6144], P('mx', 'my'), may hold values from -0.0390625 to 0.0390625
Outputs:
- teacher_out: bfloat16 [16, 257, 6144], P('dp', None, ('my', 'mx'))
The draws below stay inside these ranges and needn't reach their ends.
Inputs may be any that keep to these rules, and one draw needn't show every extreme that they name: `crop_table`: each crop is taken by exactly one slot.
All inputs are finite; a program needn't handle non-finite values.
Results may differ from the reference program's by a relative error of at most 0.018.
Values may be sent and summed in bfloat16 or wider, within the bound.
No kernel may reach another device: no remote copies, remote signals or barrier semaphores. Data moves between devices by JAX's collectives and lax.ppermute only.
A program may use at most 128 MiB of HBM per device.

```python
import math
import jax
import jax.numpy as jnp
from jax import lax

D = 6144
FF = 24576
HEADS = 48
HD = 128
TOK = 257
CROPS = 16
N_MY = 8


def draw_crops_in(key, part):
    key = jax.random.fold_in(key, 11)
    key_base, key_rough, key_rows = jax.random.split(key, 3)
    position = jnp.arange(D, dtype=jnp.float32) / D
    ramp = jnp.exp(math.log(3.0) * position)
    base = jax.random.truncated_normal(key_base, -4.0, 4.0, (CROPS, TOK, D), jnp.float32)
    rough = jnp.exp(jax.random.uniform(key_rough, (D,), jnp.float32, -0.5, 0.5))
    row_scale = jnp.exp(jax.random.uniform(key_rows, (CROPS, TOK, 1), jnp.float32, math.log(0.3), math.log(3.0)))
    return jnp.clip(base * ramp * rough * row_scale, -24.0, 24.0).astype(jnp.bfloat16)


def gain_table(key):
    return jnp.exp(jax.random.uniform(key, (HEADS, HD), jnp.float32, math.log(0.5), math.log(2.5)))


def draw_q_gain(key, part):
    key = jax.random.fold_in(key, 21)
    return gain_table(key)


def draw_k_gain(key, part):
    key = jax.random.fold_in(key, 22)
    return gain_table(key)


def level_of(own_key, dims, pieces, low, high):
    gain = 1.0
    for axis_at, parts in pieces:
        heights = jax.random.uniform(jax.random.fold_in(jax.random.fold_in(own_key, 6), axis_at), (parts,), jnp.float32, low / len(pieces), high / len(pieces))
        gain = gain * jnp.repeat(jnp.exp(heights), dims[axis_at] // parts).reshape((-1,) + (1,) * (len(dims) - 1 - axis_at))
    return gain


def centred(own_key, shape, deviation, limit, shards=(), kind=jnp.bfloat16):
    loudness = level_of(own_key, shape, shards, -0.22, 0.18) if shards else 1.0
    result = jax.random.normal(own_key, shape, jnp.float32) * deviation * loudness
    return jnp.minimum(jnp.maximum(result, -limit), limit).astype(kind)


def setup_inputs(seed: int = 0) -> dict:
    streams_of = jax.random.split(jax.random.key(seed), 11)
    crops_in = draw_crops_in(jax.random.fold_in(streams_of[10], 71), 0)
    crop_table = jax.random.permutation(streams_of[1], CROPS).astype(jnp.int32)
    ln_gain = jnp.clip(1.0 + 0.18 * jax.random.normal(streams_of[2], (D,), jnp.float32), 0.099609375, 1.8984375).astype(jnp.bfloat16)
    w_qkv = centred(streams_of[3], (D, HEADS, 3, HD), D ** -0.5, 0.078125, ((0, 8), (1, 16)))
    q_gain = draw_q_gain(jax.random.fold_in(streams_of[10], 71), 0)
    k_gain = draw_k_gain(jax.random.fold_in(streams_of[10], 71), 0)
    w_up = centred(streams_of[6], (D, FF), D ** -0.5, 0.078125, ((0, 8), (1, 16)))
    b_up = centred(streams_of[7], (FF,), 0.5, 3.0, ((0, 16),), jnp.float32)
    w_out = centred(streams_of[8], (HEADS, HD, D), D ** -0.5, 0.078125, ((0, 16), (2, 8)))
    w_down = centred(streams_of[9], (FF, D), FF ** -0.5, 0.0390625, ((0, 16), (1, 8)))
    return {"crops_in": crops_in, "crop_table": crop_table, "ln_gain": ln_gain, "w_qkv": w_qkv, "q_gain": q_gain, "k_gain": k_gain, "w_up": w_up, "b_up": b_up, "w_out": w_out, "w_down": w_down}


def head_norm(entries, gain_row):
    center = entries - lax.optimization_barrier(jnp.mean(entries, axis=-1, keepdims=True))
    spread = lax.optimization_barrier(jnp.mean(center * center, axis=-1, keepdims=True))
    return center * lax.rsqrt(spread + 1e-06) * gain_row

def attend(queries, key_rows, value_rows):
    scores = jnp.einsum('cqhd,ckhd->chqk', queries.astype(jnp.float32), key_rows.astype(jnp.float32)) / math.sqrt(queries.shape[-1])
    weights = jax.nn.softmax(scores, axis=-1).astype(jnp.bfloat16)
    mixed_out = jnp.einsum('chqk,ckhd->cqhd', weights.astype(jnp.float32), value_rows.astype(jnp.float32))
    return mixed_out.astype(jnp.bfloat16)

def grouped_product(normed, matrix):
    group_rows = D // N_MY
    running = jnp.zeros((normed.shape[0], matrix.shape[1]), jnp.float32)
    for position in range(N_MY):
        partial_value = jnp.dot(normed[:, position * group_rows:(position + 1) * group_rows], matrix[position * group_rows:(position + 1) * group_rows], preferred_element_type=jnp.float32)
        rounded = lax.optimization_barrier(partial_value.astype(jnp.bfloat16))
        running = running + rounded.astype(jnp.float32)
    return running

def reference(crops_in, crop_table, ln_gain, w_qkv, q_gain, k_gain, w_up, b_up, w_out, w_down):
    picked = jnp.take(crops_in, crop_table, axis=0)
    as_float = picked.reshape(-1, D).astype(jnp.float32)
    mean_row = lax.optimization_barrier(jnp.sum(as_float, axis=1)) / D
    var_row = lax.optimization_barrier(jnp.sum(as_float * as_float, axis=1)) / D - mean_row * mean_row
    normed = ((as_float - mean_row[:, None]) * lax.rsqrt(var_row[:, None] + 1e-06) * ln_gain.astype(jnp.float32)).astype(jnp.bfloat16)
    qkv = grouped_product(normed, w_qkv.reshape(D, -1))
    up_sums = grouped_product(normed, w_up)
    triple = qkv.reshape(CROPS, TOK, HEADS, 3, HD)
    queries = head_norm(triple[:, :, :, 0], q_gain).astype(jnp.bfloat16)
    key_rows = head_norm(triple[:, :, :, 1], k_gain).astype(jnp.bfloat16)
    value_rows = triple[:, :, :, 2].astype(jnp.bfloat16)
    attended = attend(queries, key_rows, value_rows).reshape(-1, D)
    hidden = jax.nn.gelu(up_sums + b_up, approximate=False).astype(jnp.bfloat16)
    branch_sum = jnp.dot(attended, w_out.reshape(D, D), preferred_element_type=jnp.float32) + jnp.dot(hidden, w_down, preferred_element_type=jnp.float32)
    return (as_float + branch_sum).astype(jnp.bfloat16).reshape(CROPS, TOK, D)
```

```python
import functools
import math

import jax
import jax.numpy as jnp
from jax import lax
from jax.experimental import pallas as pl
from jax.experimental.pallas import tpu as pltpu
from jax.sharding import PartitionSpec as P

D = 6144
EPS = 1e-06
F32 = jnp.float32
BF16 = jnp.bfloat16
MAIN = 256
REST = 16
ROWS = MAIN + REST
LANES = 384
LIMIT = 24 * 1024 * 1024
SMEM = pl.BlockSpec(memory_space=pltpu.SMEM)


def swap(value, axis, mask):
    count = lax.axis_size(axis)
    return lax.ppermute(value, axis, [(a, a ^ mask) for a in range(count)])


def call(kernel, outs, flops, args, scalars=0):
    size = sum(math.prod(a.shape) * a.dtype.itemsize for a in args)
    size += sum(math.prod(shape) * 2 for shape in outs)
    return pl.pallas_call(
        kernel,
        out_shape=[jax.ShapeDtypeStruct(shape, BF16) for shape in outs],
        in_specs=[SMEM] * scalars + [pl.BlockSpec(memory_space=pltpu.VMEM)] * (len(args) - scalars),
        out_specs=[pl.BlockSpec(memory_space=pltpu.VMEM)] * len(outs),
        compiler_params=pltpu.CompilerParams(vmem_limit_bytes=LIMIT),
        cost_estimate=pl.CostEstimate(flops=flops, bytes_accessed=size, transcendentals=0),
    )(*args)


def row_statistics(piece_of, count):
    first = second = 0.0
    for k in range(count):
        piece = piece_of(k)
        first = first + jnp.sum(piece, axis=1, keepdims=True)
        second = second + jnp.sum(piece * piece, axis=1, keepdims=True)
    mean = first / D
    return mean, lax.rsqrt(second / D - mean * mean + EPS)


def split_table(mean, scale):
    rows = mean.shape[0]
    lane = lax.broadcasted_iota(jnp.int32, (rows, 128), 1)
    table = jnp.zeros((rows, 128), F32)
    for k, value in ((1, mean), (4, scale)):
        for part in range(3):
            high = value.astype(BF16).astype(F32)
            table = jnp.where(lane == k + part, high, table)
            value = value - high
    return table


def pack_kernel(count, at_ref, crop_ref, last_ref, *out_refs):
    width = crop_ref.shape[1] // count
    table = split_table(
        *row_statistics(lambda k: crop_ref[:MAIN, k * width : (k + 1) * width].astype(F32), count)
    )
    final = split_table(*row_statistics(lambda k: last_ref[:, k * width : (k + 1) * width], count))
    final = jnp.where(lax.broadcasted_iota(jnp.int32, final.shape, 0) == 0, final, 0.0)
    table = jnp.concatenate([table, final, jnp.zeros((LANES - MAIN - final.shape[0], 128), F32)], axis=0)
    stats = jnp.transpose(table)[:REST]
    stats = jnp.concatenate([stats, jnp.zeros((REST, width - LANES), F32)], axis=1)
    row = lax.broadcasted_iota(jnp.int32, (REST, width), 0)
    at_y = at_ref[0]
    for k, out_ref in enumerate(out_refs):
        for c in range(out_ref.shape[0] // ROWS):
            mask = (0, 1, 4, 2, 6)[k] ^ c
            columns = pl.ds(pl.multiple_of(jnp.bitwise_xor(at_y, mask) * width, width), width)
            base = c * ROWS
            out_ref[base : base + MAIN, :] = crop_ref[:MAIN, columns]
            out_ref[base + MAIN : base + ROWS, :] = jnp.where(row == 0, last_ref[:1, columns], stats).astype(BF16)


def pack(at_y, crop, width):
    shapes = [(ROWS, width)] * 2 + [(2 * ROWS, width)] * 3
    last = jnp.pad(crop[MAIN:].astype(F32), ((0, 7), (0, 0)))
    kernel = functools.partial(pack_kernel, crop.shape[1] // width)
    return call(kernel, shapes, 6 * crop.size, [at_y, crop, last], 1)


def normalised(raw_ref, gain_ref):
    stats = raw_ref[MAIN:ROWS, :LANES].astype(F32)
    mean = (stats[1:2] + stats[2:3]) + stats[3:4]
    scale = (stats[4:5] + stats[5:6]) + stats[6:7]
    row = lax.broadcasted_iota(jnp.int32, (128, LANES), 0)
    table = jnp.where(row == 0, mean, jnp.where(row == 1, scale, 0.0))
    table = jnp.transpose(table)[:ROWS]
    return ((raw_ref[:ROWS, :].astype(F32) - table[:, :1]) * table[:, 1:2] * gain_ref[...]).astype(BF16)


def thin_columns(at_ref, raw_ref, thin_ref):
    rows, width = thin_ref.shape[0], raw_ref.shape[1]
    row = lax.broadcasted_iota(jnp.int32, (rows, width), 0)
    column = lax.broadcasted_iota(jnp.int32, (rows, width), 1)
    chosen = jnp.where(column == row + at_ref[0] * rows, 1.0, 0.0).astype(BF16)
    thin_ref[...] = lax.dot_general(
        chosen, raw_ref[:ROWS, :], (((1,), (1,)), ((), ())), preferred_element_type=F32
    ).astype(BF16)


def send_kernel(at_ref, raw_ref, gain_ref, qkv_ref, up_ref, out_ref, thin_ref):
    normed = normalised(raw_ref, gain_ref)
    at = qkv_ref.shape[1]
    for k in range(0, at, 384):
        out_ref[:, k : k + 384] = jnp.dot(normed, qkv_ref[:, k : k + 384], preferred_element_type=F32).astype(BF16)
    for k in range(0, up_ref.shape[1], 512):
        out_ref[:, at + k : at + k + 512] = jnp.dot(normed, up_ref[:, k : k + 512], preferred_element_type=F32).astype(BF16)
    thin_columns(at_ref, raw_ref, thin_ref)


def keep_kernel(at_ref, raw_ref, gain_ref, qkv_ref, up_ref, other_ref, out_qkv_ref, out_up_ref, thin_ref):
    normed = normalised(raw_ref, gain_ref)
    at = qkv_ref.shape[1]
    for k in range(0, at, 384):
        value = jnp.dot(normed, qkv_ref[:, k : k + 384], preferred_element_type=F32)
        out_qkv_ref[:, k : k + 384] = (value + other_ref[:, k : k + 384].astype(F32)).astype(BF16)
    for k in range(0, up_ref.shape[1], 512):
        value = jnp.dot(normed, up_ref[:, k : k + 512], preferred_element_type=F32)
        out_up_ref[:, k : k + 512] = (value + other_ref[:, at + k : at + k + 512].astype(F32)).astype(BF16)
    thin_columns(at_ref, raw_ref, thin_ref)


def head_norm(entries, gain_row):
    center = entries - jnp.mean(entries, axis=-1, keepdims=True)
    spread = jnp.mean(center * center, axis=-1, keepdims=True)
    return (center * lax.rsqrt(spread + EPS) * gain_row).astype(BF16)


def attend_kernel(tokens, a_ref, b_ref, c_ref, q_gain_ref, k_gain_ref, out_ref):
    heads, width = q_gain_ref.shape
    live = lax.broadcasted_iota(jnp.int32, (ROWS, LANES), 1) < tokens
    spare = jnp.zeros((LANES - ROWS, width), BF16)

    def total(at):
        part = slice(at, at + width)
        return a_ref[:, part].astype(F32) + b_ref[:, part].astype(F32) + c_ref[:, part].astype(F32)

    for h in range(heads):
        at = 3 * width * h
        queries = head_norm(total(at), q_gain_ref[h : h + 1, :])
        key_rows = jnp.concatenate([head_norm(total(at + width), k_gain_ref[h : h + 1, :]), spare], axis=0)
        value_rows = jnp.concatenate([total(at + 2 * width).astype(BF16), spare], axis=0)
        scores = lax.dot_general(
            queries, key_rows, (((1,), (1,)), ((), ())), preferred_element_type=F32
        ) / math.sqrt(width)
        scores = jnp.where(live, scores, -1e30)
        weights = jnp.exp(scores - jnp.max(scores, axis=-1, keepdims=True))
        weights = weights / jnp.sum(weights, axis=-1, keepdims=True)
        out_ref[:, width * h : width * (h + 1)] = jnp.dot(
            weights.astype(BF16), value_rows, preferred_element_type=F32
        ).astype(BF16)


def hidden_kernel(a_ref, b_ref, c_ref, bias_ref, attended_ref, out_ref):
    at = attended_ref.shape[1]
    out_ref[:, :at] = attended_ref[...]
    for k in range(0, a_ref.shape[1], 256):
        part = slice(k, k + 256)
        value = a_ref[:, part].astype(F32) + b_ref[:, part].astype(F32) + c_ref[:, part].astype(F32)
        value = value + bias_ref[:, part]
        value = 0.5 * value * (1.0 + lax.erf(value * math.sqrt(0.5)))
        out_ref[:, at + k : at + k + 256] = value.astype(BF16)


def out_kernel(crops, matrix_ref, *refs):
    out_refs = refs[-4:]
    pieces = list(refs[:-4])
    step = matrix_ref.shape[0] // 4

    def product(rows, at, size):
        for k, out_ref in enumerate(out_refs):
            out_ref[:, at : at + size] = lax.dot_general(
                matrix_ref[k * step : (k + 1) * step, :], rows, (((1,), (1,)), ((), ())), preferred_element_type=F32
            ).astype(BF16)

    at = 0
    for parts in crops:
        rows = [pieces.pop(0) for _ in range(parts)]
        if parts == 1:
            product(rows[0][:MAIN, :], at, MAIN)
        else:
            product(jnp.concatenate([rows[0][...], rows[1][: MAIN - rows[0].shape[0], :]], axis=0), at, MAIN)
        at += MAIN
    if pieces:
        product(pieces[0][...], at, pieces[0].shape[0])


def project_out(matrix, crops, rest):
    pieces = [p for crop in crops for p in crop] + ([rest] if rest is not None else [])
    length = MAIN * len(crops) + (rest.shape[0] if rest is not None else 0)
    width, depth = matrix.shape
    kernel = functools.partial(out_kernel, [len(crop) for crop in crops])
    return call(kernel, [(width // 4, length)] * 4, 2 * width * depth * length, [matrix] + pieces)


def middle_kernel(a_ref, b_ref, c_ref, d_ref, *out_refs):
    step = out_refs[0].shape[0]
    for k, out_ref in enumerate(out_refs):
        part = slice(k * step, (k + 1) * step)
        out_ref[...] = (
            a_ref[part, :].astype(F32) + b_ref[part, :].astype(F32) + c_ref[part, :].astype(F32) + d_ref[part, :].astype(F32)
        ).astype(BF16)


def middle(terms):
    rows, length = terms[0].shape
    return call(middle_kernel, [(rows // 4, length)] * 4, 4 * rows * length, list(terms))


def shards(crops_in, crop_table, ln_gain, w_qkv, q_gain, k_gain, w_up, b_up, w_out, w_down):
    _, tokens, model_width = crops_in.shape
    count_y = lax.axis_size("my")
    count_x = lax.axis_size("mx")
    at_y = lax.axis_index("my")
    at_m = lax.axis_index("mx")
    at_d = lax.axis_index("dp")
    width = model_width // count_y
    thin = width // count_x
    heads_local, head_dim = w_out.shape[0], w_out.shape[1]
    split_at = heads_local * head_dim

    mine, beside, far, near, back = pack(at_y.astype(jnp.int32).reshape(1), crops_in[0], width)
    raw = [None] * 4
    raw[0] = (mine, swap(beside, "my", 1))
    got = swap(far, "my", 4)
    got, near, back = lax.optimization_barrier((got, near, back))
    raw[2] = (got, swap(got[ROWS:], "my", 1))
    for k, value in ((1, near), (3, back)):
        got = swap(value, "my", 2 * k)
        raw[k] = (got, swap(got[ROWS:], "my", 1))

    weights_qkv = w_qkv.reshape(width, -1)
    gain = ln_gain.astype(F32).reshape(1, width)
    columns = weights_qkv.shape[1] + w_up.shape[1]
    flops = 2 * ROWS * width * columns
    terms_qkv, terms_up, resid = [None] * 4, [None] * 4, [None] * count_y
    place = at_m.astype(jnp.int32).reshape(1)
    for k in (2, 1, 3, 0):
        other, resid[2 * k + 1] = call(
            send_kernel,
            [(ROWS, columns), (thin, ROWS)],
            flops,
            [place, raw[k][1], gain, weights_qkv, w_up],
            1,
        )
        other = swap(other, "my", 1)
        terms_qkv[k], terms_up[k], resid[2 * k] = call(
            keep_kernel,
            [(ROWS, weights_qkv.shape[1]), (ROWS, w_up.shape[1]), (thin, ROWS)],
            flops,
            [place, raw[k][0], gain, weights_qkv, w_up, other],
            1,
        )

    def add(one, two):
        return (one.astype(F32) + two.astype(F32)).astype(BF16)

    far_qkv = swap(terms_qkv[2], "my", 2)
    far_up = swap(terms_up[2], "my", 6)
    near_qkv = swap(terms_qkv[1], "my", 2)
    back_qkv = swap(add(terms_qkv[3], far_qkv), "my", 6)
    back_up = swap(terms_up[3], "my", 6)
    near_up = swap(add(terms_up[1], far_up), "my", 2)

    (attended,) = call(
        functools.partial(attend_kernel, tokens),
        [(ROWS, split_at)],
        4 * ROWS * ROWS * split_at,
        [terms_qkv[0], near_qkv, back_qkv, q_gain, k_gain],
    )
    hidden_width = w_up.shape[1]
    (branch,) = call(
        hidden_kernel,
        [(ROWS, split_at + hidden_width)],
        40 * ROWS * hidden_width,
        [terms_up[0], near_up, back_up, b_up.reshape(1, -1), attended],
    )

    cut = 128
    near_branch = swap(branch, "my", 2)
    back_branch = swap(branch, "my", 6)
    far_lead = swap(back_branch[:cut], "my", 2)
    far_trail = swap(near_branch[cut:], "my", 6)
    found = {0: (branch,), 1: (near_branch,), 3: (back_branch,), 2: (far_lead, far_trail)}
    pieces = [None] * count_y
    for k in (0, 1, 3, 2):
        pieces[2 * k] = found[k]
        pieces[2 * k + 1] = tuple(swap(p, "my", 1) for p in found[k])

    matrix = jnp.concatenate([w_out.reshape(split_at, width).T, w_down.T], axis=1).reshape(count_x, thin, -1)
    order = jnp.bitwise_xor(at_m, jnp.arange(count_x, dtype=jnp.int32))
    matrix = jnp.take(matrix, order, axis=0, mode="clip").reshape(width, -1)

    final_main = [None] * count_y
    final_rest = None
    for blocks in ((0, 1), (2, 3, 6, 7), (4, 5)):
        rest = None
        base = [resid[r][:, :MAIN] for r in blocks]
        if blocks[0] == 4:
            rest = jnp.concatenate([pieces[r][-1][-REST:] for r in range(count_y)], axis=0)
            base += [resid[r][:, MAIN:] for r in range(count_y)]
        parts = project_out(matrix, [pieces[r] for r in blocks], rest)
        parts = [parts[0]] + [swap(parts[k], "mx", 4 * k) for k in (1, 2, 3)]
        parts = middle(parts)
        parts = [parts[0]] + [swap(parts[k], "mx", k) for k in (1, 2, 3)]
        own = sum(p.astype(F32) for p in parts)
        own = (own + jnp.concatenate(base, axis=1).astype(F32)).astype(BF16)
        both = jnp.stack([own, swap(own, "dp", 1)])
        for k, r in enumerate(blocks):
            final_main[r] = both[:, :, k * MAIN : (k + 1) * MAIN]
        if rest is not None:
            final_rest = both[:, :, len(blocks) * MAIN :]

    whole = jnp.stack(final_main, axis=1).reshape(2 * count_y, thin, MAIN)
    final_rest = final_rest.reshape(2, thin, count_y, REST)[:, :, :, :1]
    final_rest = final_rest.transpose(0, 2, 1, 3).reshape(2 * count_y, thin, 1)
    chosen = lax.dynamic_slice_in_dim(crop_table, at_d * count_y, count_y)
    place = jnp.bitwise_xor(chosen // count_y, at_d) * count_y + jnp.bitwise_xor(chosen % count_y, at_y)
    result = jnp.concatenate([jnp.take(whole, place, axis=0), jnp.take(final_rest, place, axis=0)], axis=2)
    return result.transpose(0, 2, 1)


def solution(mesh):
    placed = (
        P(("dp", "my"), None, None),
        P(),
        P("my"),
        P("my", "mx", None, None),
        P("mx", None),
        P("mx", None),
        P("my", "mx"),
        P("mx"),
        P("mx", None, "my"),
        P("mx", "my"),
    )
    return jax.shard_map(
        shards, mesh=mesh, in_specs=placed, out_specs=P("dp", None, ("my", "mx")), check_vma=False
    )
```

```python
import functools
import math

import jax
import jax.numpy as jnp
from jax import lax
from jax.experimental import pallas as pl
from jax.experimental.pallas import tpu as pltpu
from jax.sharding import PartitionSpec as P

D = 6144
EPS = 1e-06
F32 = jnp.float32
BF16 = jnp.bfloat16
MAIN = 256
REST = 16
ROWS = MAIN + REST
LANES = 384
PACKED = ((5,), (4,), (3,), (7,), (2,), (6,), (1,), (0,))
LIMIT = 16 * 1024 * 1024
SMEM = pl.BlockSpec(memory_space=pltpu.SMEM)


def swap(value, axis, mask):
    count = lax.axis_size(axis)
    return lax.ppermute(value, axis, [(a, a ^ mask) for a in range(count)])


def call(kernel, outs, args, scalars=0):
    return pl.pallas_call(
        kernel,
        out_shape=[jax.ShapeDtypeStruct(shape, BF16) for shape in outs],
        in_specs=[SMEM] * scalars + [pl.BlockSpec(memory_space=pltpu.VMEM)] * (len(args) - scalars),
        out_specs=[pl.BlockSpec(memory_space=pltpu.VMEM)] * len(outs),
        compiler_params=pltpu.CompilerParams(vmem_limit_bytes=LIMIT),
        cost_estimate=pl.CostEstimate(flops=1000, bytes_accessed=1000, transcendentals=0),
    )(*args)


def row_statistics(piece_of, count):
    first = second = 0.0
    for k in range(count):
        piece = piece_of(k)
        first = first + jnp.sum(piece, axis=1, keepdims=True)
        second = second + jnp.sum(piece * piece, axis=1, keepdims=True)
    mean = first / D
    return mean, lax.rsqrt(second / D - mean * mean + EPS)


def split_table(mean, scale):
    rows = mean.shape[0]
    lane = lax.broadcasted_iota(jnp.int32, (rows, 128), 1)
    table = jnp.zeros((rows, 128), F32)
    for k, value in ((1, mean), (4, scale)):
        for part in range(3):
            high = value.astype(BF16).astype(F32)
            table = jnp.where(lane == k + part, high, table)
            value = value - high
    return table


def pack_kernel(count, at_ref, crop_ref, last_ref, *out_refs):
    width = crop_ref.shape[1] // count
    table = split_table(
        *row_statistics(lambda k: crop_ref[:MAIN, k * width : (k + 1) * width].astype(F32), count)
    )
    final = split_table(*row_statistics(lambda k: last_ref[:, k * width : (k + 1) * width], count))
    final = jnp.where(lax.broadcasted_iota(jnp.int32, final.shape, 0) == 0, final, 0.0)
    table = jnp.concatenate([table, final, jnp.zeros((LANES - MAIN - final.shape[0], 128), F32)], axis=0)
    stats = jnp.transpose(table)[:REST]
    stats = jnp.concatenate([stats, jnp.zeros((REST, width - LANES), F32)], axis=1)
    row = lax.broadcasted_iota(jnp.int32, (REST, width), 0)
    at_y = at_ref[0]
    for out_ref, masks in zip(out_refs, PACKED):
        for k, mask in enumerate(masks):
            columns = pl.ds(pl.multiple_of(jnp.bitwise_xor(at_y, mask) * width, width), width)
            base = k * ROWS
            out_ref[base : base + MAIN, :] = crop_ref[:MAIN, columns]
            out_ref[base + MAIN : base + ROWS, :] = jnp.where(row == 0, last_ref[:1, columns], stats).astype(BF16)


def pack(at_y, crop, width):
    shapes = [(ROWS * len(masks), width) for masks in PACKED]
    last = jnp.pad(crop[MAIN:].astype(F32), ((0, 7), (0, 0)))
    kernel = functools.partial(pack_kernel, crop.shape[1] // width)
    return call(kernel, shapes, [at_y, crop, last], 1)


def normalised(raw_ref, gain_ref):
    stats = raw_ref[MAIN:ROWS, :LANES].astype(F32)
    mean = (stats[1:2] + stats[2:3]) + stats[3:4]
    scale = (stats[4:5] + stats[5:6]) + stats[6:7]
    row = lax.broadcasted_iota(jnp.int32, (128, LANES), 0)
    table = jnp.where(row == 0, mean, jnp.where(row == 1, scale, 0.0))
    table = jnp.transpose(table)[:ROWS]
    return ((raw_ref[:ROWS, :].astype(F32) - table[:, :1]) * table[:, 1:2] * gain_ref[...]).astype(BF16)


def thin_columns(at_ref, raw_ref, thin_ref):
    rows, width = thin_ref.shape[0], raw_ref.shape[1]
    row = lax.broadcasted_iota(jnp.int32, (rows, width), 0)
    column = lax.broadcasted_iota(jnp.int32, (rows, width), 1)
    chosen = jnp.where(column == row + at_ref[0] * rows, 1.0, 0.0).astype(BF16)
    thin_ref[...] = lax.dot_general(
        chosen, raw_ref[:ROWS, :], (((1,), (1,)), ((), ())), preferred_element_type=F32
    ).astype(BF16)


def products(normed, qkv_ref, up_ref):
    blocks, _, size = qkv_ref.shape
    for k in range(0, blocks, 3):
        matrix = jnp.concatenate([qkv_ref[k], qkv_ref[k + 1], qkv_ref[k + 2]], axis=1)
        yield k * size, jnp.dot(normed, matrix, preferred_element_type=F32)
    for k in range(0, up_ref.shape[1], 768):
        yield blocks * size + k, jnp.dot(normed, up_ref[:, k : k + 768], preferred_element_type=F32)


def send_kernel(at_ref, raw_ref, gain_ref, qkv_ref, up_ref, out_ref, thin_ref):
    for at, value in products(normalised(raw_ref, gain_ref), qkv_ref, up_ref):
        out_ref[:, at : at + value.shape[1]] = value.astype(BF16)
    thin_columns(at_ref, raw_ref, thin_ref)


def keep_kernel(at_ref, raw_ref, gain_ref, qkv_ref, up_ref, other_ref, *refs):
    out_refs, thin_ref = list(refs[:-1]), refs[-1]
    base = 0
    for at, value in products(normalised(raw_ref, gain_ref), qkv_ref, up_ref):
        size = value.shape[1]
        if at - base == out_refs[0].shape[1]:
            base += out_refs.pop(0).shape[1]
        value = value + other_ref[:, at : at + size].astype(F32)
        out_refs[0][:, at - base : at - base + size] = value.astype(BF16)
    thin_columns(at_ref, raw_ref, thin_ref)


def add_kernel(one_ref, two_ref, out_ref):
    out_ref[...] = (one_ref[...].astype(F32) + two_ref[...].astype(F32)).astype(BF16)


def head_norm(entries, gain_row):
    center = entries - jnp.mean(entries, axis=-1, keepdims=True)
    spread = jnp.mean(center * center, axis=-1, keepdims=True)
    return (center * lax.rsqrt(spread + EPS) * gain_row).astype(BF16)


def attend_kernel(tokens, a_ref, b_ref, c_ref, q_gain_ref, k_gain_ref, out_ref):
    heads, width = q_gain_ref.shape
    live = lax.broadcasted_iota(jnp.int32, (ROWS, LANES), 1) < tokens
    spare = jnp.zeros((LANES - ROWS, width), BF16)

    def total(at):
        part = slice(at, at + width)
        return a_ref[:, part].astype(F32) + b_ref[:, part].astype(F32) + c_ref[:, part].astype(F32)

    for h in range(heads):
        at = 3 * width * h
        queries = head_norm(total(at), q_gain_ref[h : h + 1, :])
        key_rows = jnp.concatenate([head_norm(total(at + width), k_gain_ref[h : h + 1, :]), spare], axis=0)
        value_rows = jnp.concatenate([total(at + 2 * width).astype(BF16), spare], axis=0)
        scores = lax.dot_general(
            queries, key_rows, (((1,), (1,)), ((), ())), preferred_element_type=F32
        ) / math.sqrt(width)
        scores = jnp.where(live, scores, -1e30)
        weights = jnp.exp(scores - jnp.max(scores, axis=-1, keepdims=True))
        weights = weights / jnp.sum(weights, axis=-1, keepdims=True)
        out_ref[:, width * h : width * (h + 1)] = jnp.dot(
            weights.astype(BF16), value_rows, preferred_element_type=F32
        ).astype(BF16)


def hidden_kernel(a_ref, b_ref, c_ref, bias_ref, attended_ref, out_ref):
    at = attended_ref.shape[1]
    out_ref[:, :at] = attended_ref[...]
    for k in range(0, a_ref.shape[1], 256):
        part = slice(k, k + 256)
        value = a_ref[:, part].astype(F32) + b_ref[:, part].astype(F32) + c_ref[:, part].astype(F32)
        value = value + bias_ref[:, part]
        value = 0.5 * value * (1.0 + lax.erf(value * math.sqrt(0.5)))
        out_ref[:, at + k : at + k + 256] = value.astype(BF16)


def out_kernel(crops, matrix_ref, *refs):
    out_refs = refs[-4:]
    pieces = list(refs[:-4])
    step = matrix_ref.shape[0] // 4

    def product(rows, at, size):
        for k, out_ref in enumerate(out_refs):
            out_ref[:, at : at + size] = lax.dot_general(
                matrix_ref[k * step : (k + 1) * step, :], rows, (((1,), (1,)), ((), ())), preferred_element_type=F32
            ).astype(BF16)

    at = 0
    for parts in crops:
        rows = [pieces.pop(0) for _ in range(parts)]
        if parts == 1:
            product(rows[0][:MAIN, :], at, MAIN)
        else:
            product(jnp.concatenate([rows[0][...], rows[1][: MAIN - rows[0].shape[0], :]], axis=0), at, MAIN)
        at += MAIN
    if pieces:
        product(pieces[0][...], at, pieces[0].shape[0])


def project_out(matrix, crops, rest):
    pieces = [p for crop in crops for p in crop] + ([rest] if rest is not None else [])
    length = MAIN * len(crops) + (rest.shape[0] if rest is not None else 0)
    width = matrix.shape[0]
    kernel = functools.partial(out_kernel, [len(crop) for crop in crops])
    return call(kernel, [(width // 4, length)] * 4, [matrix] + pieces)


def middle_kernel(a_ref, b_ref, c_ref, d_ref, *out_refs):
    step = out_refs[0].shape[0]
    for k, out_ref in enumerate(out_refs):
        part = slice(k * step, (k + 1) * step)
        out_ref[...] = (
            a_ref[part, :].astype(F32) + b_ref[part, :].astype(F32) + c_ref[part, :].astype(F32) + d_ref[part, :].astype(F32)
        ).astype(BF16)


def middle(terms):
    rows, length = terms[0].shape
    return call(middle_kernel, [(rows // 4, length)] * 4, list(terms))


def final_kernel(count, with_rest, *refs):
    terms, resid_refs, out_ref = refs[:4], refs[4:-1], refs[-1]

    def total(part):
        return terms[0][:, part].astype(F32) + terms[1][:, part].astype(F32) + terms[2][:, part].astype(F32) + terms[3][:, part].astype(F32)

    for k in range(count):
        part = slice(k * MAIN, (k + 1) * MAIN)
        out_ref[:, part] = (total(part) + resid_refs[k][:, :MAIN].astype(F32)).astype(BF16)
    if with_rest:
        part = slice(count * MAIN, count * MAIN + REST * len(resid_refs[count:]))
        rest = jnp.concatenate([ref[:, MAIN:].astype(F32) for ref in resid_refs[count:]], axis=1)
        out_ref[:, part] = (total(part) + rest).astype(BF16)


CHUNKS = ((0, 1), (2, 3, 6, 7), (4, 5))


def place_kernel(place_ref, *refs):
    out_ref, main_ref, rest_ref = refs[6:]
    count, thin, _ = out_ref.shape
    for d in range(2):
        parts = refs[3 * d : 3 * d + 3]
        for ref, blocks in zip(parts, CHUNKS):
            for k, r in enumerate(blocks):
                main_ref[count * d + r] = ref[:, k * MAIN : (k + 1) * MAIN].astype(F32)
        last = parts[2][:, 2 * MAIN :].astype(F32)
        for r in range(count):
            rest_ref[count * d + r] = jnp.broadcast_to(last[:, REST * r : REST * r + 1], (thin, 128))
    for slot in range(count):
        at = place_ref[slot]
        out_ref[slot, :, :MAIN] = main_ref[at].astype(BF16)
        out_ref[slot, :, MAIN:] = rest_ref[at][:, :1].astype(BF16)


def shards(crops_in, crop_table, ln_gain, w_qkv, q_gain, k_gain, w_up, b_up, w_out, w_down):
    _, tokens, model_width = crops_in.shape
    count_y = lax.axis_size("my")
    count_x = lax.axis_size("mx")
    at_y = lax.axis_index("my")
    at_m = lax.axis_index("mx")
    at_d = lax.axis_index("dp")
    width = model_width // count_y
    thin = width // count_x
    heads_local, head_dim = w_out.shape[0], w_out.shape[1]
    split_at = heads_local * head_dim
    hidden_width = w_up.shape[1]

    far_a, far_b, near_a, back_a, near_b, back_b, beside, mine = pack(
        at_y.astype(jnp.int32).reshape(1), crops_in[0], width
    )
    barrier = lax.optimization_barrier
    far_a = swap(far_a, "my", 5)
    far_b = swap(far_b, "my", 4)

    matrix = jnp.concatenate([w_out.reshape(split_at, width).T, w_down.T], axis=1).reshape(count_x, thin, -1)
    order = jnp.bitwise_xor(at_m, jnp.arange(count_x, dtype=jnp.int32))
    matrix = jnp.take(matrix, order, axis=0, mode="clip").reshape(width, -1)
    far_a, far_b, matrix, near_a, back_a, near_b, back_b = barrier((far_a, far_b, matrix, near_a, back_a, near_b, back_b))
    near_a, back_a, near_b, back_b = barrier(
        (swap(near_a, "my", 3), swap(back_a, "my", 7), swap(near_b, "my", 2), swap(back_b, "my", 6))
    )

    qkv_width = 3 * split_at
    weights_qkv = w_qkv.transpose(1, 2, 0, 3).reshape(3 * heads_local, width, head_dim)
    gain = ln_gain.astype(F32).reshape(1, width)
    resid = [None] * count_y
    place = at_m.astype(jnp.int32).reshape(1)

    def send(k, raw):
        other, resid[2 * k + 1] = call(
            send_kernel, [(ROWS, qkv_width + hidden_width), (thin, ROWS)], [place, raw, gain, weights_qkv, w_up], 1
        )
        return swap(other, "my", 1)

    def keep(k, raw, other):
        *terms, resid[2 * k] = call(
            keep_kernel,
            [(ROWS, qkv_width), (ROWS, hidden_width), (thin, ROWS)],
            [place, raw, gain, weights_qkv, w_up, other],
            1,
        )
        return terms

    def add(one, two):
        return call(add_kernel, [one.shape], [one, two])[0]

    far_other = send(2, far_a)
    far_parts = keep(2, far_b, far_other)
    far_qkv = swap(far_parts[0], "my", 2)
    far_up = swap(far_parts[1], "my", 6)
    beside, mine, _ = barrier((beside, mine, far_parts[0]))
    own_qkv, own_up = keep(0, mine, send(0, swap(beside, "my", 1)))
    near_a, back_a, _ = barrier((near_a, back_a, far_parts[0]))
    near_other = send(1, near_a)
    back_other = send(3, back_a)
    near_qkv, near_up = keep(1, near_b, near_other)
    near_qkv = swap(near_qkv, "my", 2)
    back_qkv, back_up = keep(3, back_b, back_other)
    back_qkv = swap(add(back_qkv, far_qkv), "my", 6)
    near_up, _ = barrier((add(near_up, far_up), near_qkv))
    near_up = swap(near_up, "my", 2)
    back_up, _ = barrier((back_up, back_qkv))
    back_up = swap(back_up, "my", 6)

    (attended,) = call(
        functools.partial(attend_kernel, tokens),
        [(ROWS, split_at)],
        [own_qkv, near_qkv, back_qkv, q_gain, k_gain],
    )
    (branch,) = call(
        hidden_kernel,
        [(ROWS, split_at + hidden_width)],
        [own_up, near_up, back_up, b_up.reshape(1, -1), attended],
    )

    cut = 128
    near_branch = swap(branch, "my", 2)
    back_branch = swap(branch, "my", 6)
    beside_branch = swap(branch, "my", 1)

    def output(blocks, crops, rest):
        parts = project_out(matrix, crops, rest)
        first = parts[0]
        parts = [parts[0]] + [swap(parts[k], "mx", 4 * k) for k in (1, 2, 3)]
        parts = middle(parts)
        second = parts[0]
        parts = [parts[0]] + [swap(parts[k], "mx", k) for k in (1, 2, 3)]
        base = [resid[r] for r in blocks] + (resid if rest is not None else [])
        (own,) = call(
            functools.partial(final_kernel, len(blocks), rest is not None),
            [parts[0].shape],
            list(parts) + base,
        )
        return first, second, own, swap(own, "dp", 1)

    _, second, own_0, other_0 = output(CHUNKS[0], [(branch,), (beside_branch,)], None)
    near_branch, back_branch, _ = barrier((near_branch, back_branch, second))
    far_lead = swap(back_branch[:cut], "my", 2)
    far_trail = swap(near_branch[cut:], "my", 6)
    near_side = swap(near_branch, "my", 1)
    back_side = swap(back_branch, "my", 1)
    first, _, own_1, other_1 = output(CHUNKS[1], [(near_branch,), (near_side,), (back_branch,), (back_side,)], None)
    far_lead, far_trail, _, _ = barrier((far_lead, far_trail, first, own_0))
    far_lead_side = swap(far_lead, "my", 1)
    far_trail_side = swap(far_trail, "my", 1)
    rest = jnp.concatenate(
        [
            piece[-REST:]
            for piece in (branch, beside_branch, near_branch, near_side, far_trail, far_trail_side, back_branch, back_side)
        ],
        axis=0,
    )
    _, _, own_2, other_2 = output(CHUNKS[2], [(far_lead, far_trail), (far_lead_side, far_trail_side)], rest)

    chosen = lax.dynamic_slice_in_dim(crop_table, at_d * count_y, count_y)
    place = jnp.bitwise_xor(chosen // count_y, at_d) * count_y + jnp.bitwise_xor(chosen % count_y, at_y)
    result = pl.pallas_call(
        place_kernel,
        out_shape=jax.ShapeDtypeStruct((count_y, thin, tokens), BF16),
        in_specs=[SMEM] + [pl.BlockSpec(memory_space=pltpu.VMEM)] * 6,
        out_specs=pl.BlockSpec(memory_space=pltpu.VMEM),
        scratch_shapes=[pltpu.VMEM((2 * count_y, thin, MAIN), F32), pltpu.VMEM((2 * count_y, thin, 128), F32)],
        compiler_params=pltpu.CompilerParams(vmem_limit_bytes=LIMIT),
        cost_estimate=pl.CostEstimate(flops=1000, bytes_accessed=1000, transcendentals=0),
    )(place.astype(jnp.int32), own_0, own_1, own_2, other_0, other_1, other_2)
    return result.transpose(0, 2, 1)


def solution(mesh):
    placed = (
        P(("dp", "my"), None, None),
        P(),
        P("my"),
        P("my", "mx", None, None),
        P("mx", None),
        P("mx", None),
        P("my", "mx"),
        P("mx"),
        P("mx", None, "my"),
        P("mx", "my"),
    )
    return jax.shard_map(
        shards, mesh=mesh, in_specs=placed, out_specs=P("dp", None, ("my", "mx")), check_vma=False
    )
```

```python
import functools
import math

import jax
import jax.numpy as jnp
from jax import lax
from jax.experimental import pallas as pl
from jax.experimental.pallas import tpu as pltpu
from jax.sharding import PartitionSpec as P

D = 6144
EPS = 1e-06
F32 = jnp.float32
BF16 = jnp.bfloat16
MAIN = 256
REST = 16
ROWS = MAIN + REST
LANES = 384
FIRST = (5, 4)
SECOND = (3, 7, 2, 6, 1, 0)
LIMIT = 16 * 1024 * 1024
SMEM = pl.BlockSpec(memory_space=pltpu.SMEM)


def swap(value, axis, mask):
    count = lax.axis_size(axis)
    return lax.ppermute(value, axis, [(a, a ^ mask) for a in range(count)])


def call(kernel, outs, args, scalars=0):
    return pl.pallas_call(
        kernel,
        out_shape=[jax.ShapeDtypeStruct(shape, BF16) for shape in outs],
        in_specs=[SMEM] * scalars + [pl.BlockSpec(memory_space=pltpu.VMEM)] * (len(args) - scalars),
        out_specs=[pl.BlockSpec(memory_space=pltpu.VMEM)] * len(outs),
        compiler_params=pltpu.CompilerParams(vmem_limit_bytes=LIMIT),
        cost_estimate=pl.CostEstimate(flops=1000, bytes_accessed=1000, transcendentals=0),
    )(*args)


def row_statistics(piece_of, count):
    first = second = 0.0
    for k in range(count):
        piece = piece_of(k)
        first = first + jnp.sum(piece, axis=1, keepdims=True)
        second = second + jnp.sum(piece * piece, axis=1, keepdims=True)
    mean = first / D
    return mean, lax.rsqrt(second / D - mean * mean + EPS)


def split_table(mean, scale):
    rows = mean.shape[0]
    lane = lax.broadcasted_iota(jnp.int32, (rows, 128), 1)
    table = jnp.zeros((rows, 128), F32)
    for k, value in ((1, mean), (4, scale)):
        for part in range(3):
            high = value.astype(BF16).astype(F32)
            table = jnp.where(lane == k + part, high, table)
            value = value - high
    return table


def pack_kernel(count, masks, at_ref, crop_ref, last_ref, *out_refs):
    width = crop_ref.shape[1] // count
    table = split_table(
        *row_statistics(lambda k: crop_ref[:MAIN, k * width : (k + 1) * width].astype(F32), count)
    )
    final = split_table(*row_statistics(lambda k: last_ref[:, k * width : (k + 1) * width], count))
    final = jnp.where(lax.broadcasted_iota(jnp.int32, final.shape, 0) == 0, final, 0.0)
    table = jnp.concatenate([table, final, jnp.zeros((LANES - MAIN - final.shape[0], 128), F32)], axis=0)
    stats = jnp.transpose(table)[:REST]
    stats = jnp.concatenate([stats, jnp.zeros((REST, width - LANES), F32)], axis=1)
    row = lax.broadcasted_iota(jnp.int32, (REST, width), 0)
    at_y = at_ref[0]
    for out_ref, mask in zip(out_refs, masks):
        columns = pl.ds(pl.multiple_of(jnp.bitwise_xor(at_y, mask) * width, width), width)
        out_ref[:MAIN, :] = crop_ref[:MAIN, columns]
        out_ref[MAIN:, :] = jnp.where(row == 0, last_ref[:1, columns], stats).astype(BF16)


def pack(at_y, crop, last, width, masks):
    kernel = functools.partial(pack_kernel, crop.shape[1] // width, masks)
    return call(kernel, [(ROWS, width)] * len(masks), [at_y, crop, last], 1)


def normalised(raw_ref, gain_ref):
    stats = raw_ref[MAIN:ROWS, :LANES].astype(F32)
    mean = (stats[1:2] + stats[2:3]) + stats[3:4]
    scale = (stats[4:5] + stats[5:6]) + stats[6:7]
    row = lax.broadcasted_iota(jnp.int32, (128, LANES), 0)
    table = jnp.where(row == 0, mean, jnp.where(row == 1, scale, 0.0))
    table = jnp.transpose(table)[:ROWS]
    return ((raw_ref[:ROWS, :].astype(F32) - table[:, :1]) * table[:, 1:2] * gain_ref[...]).astype(BF16)


def thin_columns(at_ref, raw_ref, thin_ref):
    rows, width = thin_ref.shape[0], raw_ref.shape[1]
    row = lax.broadcasted_iota(jnp.int32, (rows, width), 0)
    column = lax.broadcasted_iota(jnp.int32, (rows, width), 1)
    chosen = jnp.where(column == row + at_ref[0] * rows, 1.0, 0.0).astype(BF16)
    thin_ref[...] = lax.dot_general(
        chosen, raw_ref[:ROWS, :], (((1,), (1,)), ((), ())), preferred_element_type=F32
    ).astype(BF16)


def products(normed, qkv_ref, up_ref):
    blocks, _, size = qkv_ref.shape
    for k in range(0, blocks, 3):
        matrix = jnp.concatenate([qkv_ref[k], qkv_ref[k + 1], qkv_ref[k + 2]], axis=1)
        yield k * size, jnp.dot(normed, matrix, preferred_element_type=F32)
    for k in range(0, up_ref.shape[1], 768):
        yield blocks * size + k, jnp.dot(normed, up_ref[:, k : k + 768], preferred_element_type=F32)


def send_kernel(at_ref, raw_ref, gain_ref, qkv_ref, up_ref, out_ref, thin_ref):
    for at, value in products(normalised(raw_ref, gain_ref), qkv_ref, up_ref):
        out_ref[:, at : at + value.shape[1]] = value.astype(BF16)
    thin_columns(at_ref, raw_ref, thin_ref)


def keep_kernel(at_ref, raw_ref, gain_ref, qkv_ref, up_ref, other_ref, *refs):
    out_refs, thin_ref = list(refs[:-1]), refs[-1]
    base = 0
    for at, value in products(normalised(raw_ref, gain_ref), qkv_ref, up_ref):
        size = value.shape[1]
        if at - base == out_refs[0].shape[1]:
            base += out_refs.pop(0).shape[1]
        value = value + other_ref[:, at : at + size].astype(F32)
        out_refs[0][:, at - base : at - base + size] = value.astype(BF16)
    thin_columns(at_ref, raw_ref, thin_ref)


def add_kernel(one_ref, two_ref, out_ref):
    out_ref[...] = (one_ref[...].astype(F32) + two_ref[...].astype(F32)).astype(BF16)


def head_norm(entries, gain_row):
    center = entries - jnp.mean(entries, axis=-1, keepdims=True)
    spread = jnp.mean(center * center, axis=-1, keepdims=True)
    return (center * lax.rsqrt(spread + EPS) * gain_row).astype(BF16)


def attend_kernel(tokens, a_ref, b_ref, c_ref, q_gain_ref, k_gain_ref, out_ref):
    heads, width = q_gain_ref.shape
    live = lax.broadcasted_iota(jnp.int32, (ROWS, LANES), 1) < tokens
    spare = jnp.zeros((LANES - ROWS, width), BF16)

    def total(at):
        part = slice(at, at + width)
        return a_ref[:, part].astype(F32) + b_ref[:, part].astype(F32) + c_ref[:, part].astype(F32)

    for h in range(heads):
        at = 3 * width * h
        queries = head_norm(total(at), q_gain_ref[h : h + 1, :])
        key_rows = jnp.concatenate([head_norm(total(at + width), k_gain_ref[h : h + 1, :]), spare], axis=0)
        value_rows = jnp.concatenate([total(at + 2 * width).astype(BF16), spare], axis=0)
        scores = lax.dot_general(
            queries, key_rows, (((1,), (1,)), ((), ())), preferred_element_type=F32
        ) / math.sqrt(width)
        scores = jnp.where(live, scores, -1e30)
        weights = jnp.exp(scores - jnp.max(scores, axis=-1, keepdims=True))
        weights = weights / jnp.sum(weights, axis=-1, keepdims=True)
        out_ref[:, width * h : width * (h + 1)] = jnp.dot(
            weights.astype(BF16), value_rows, preferred_element_type=F32
        ).astype(BF16)


def hidden_kernel(a_ref, b_ref, c_ref, bias_ref, attended_ref, out_ref):
    at = attended_ref.shape[1]
    out_ref[:, :at] = attended_ref[...]
    for k in range(0, a_ref.shape[1], 256):
        part = slice(k, k + 256)
        value = a_ref[:, part].astype(F32) + b_ref[:, part].astype(F32) + c_ref[:, part].astype(F32)
        value = value + bias_ref[:, part]
        value = 0.5 * value * (1.0 + lax.erf(value * math.sqrt(0.5)))
        out_ref[:, at + k : at + k + 256] = value.astype(BF16)


def out_kernel(crops, matrix_ref, *refs):
    out_refs = refs[-4:]
    pieces = list(refs[:-4])
    step = matrix_ref.shape[0] // 4

    def product(rows, at, size):
        for k, out_ref in enumerate(out_refs):
            out_ref[:, at : at + size] = lax.dot_general(
                matrix_ref[k * step : (k + 1) * step, :], rows, (((1,), (1,)), ((), ())), preferred_element_type=F32
            ).astype(BF16)

    at = 0
    for parts in crops:
        rows = [pieces.pop(0) for _ in range(parts)]
        if parts == 1:
            product(rows[0][:MAIN, :], at, MAIN)
        else:
            product(jnp.concatenate([rows[0][...], rows[1][: MAIN - rows[0].shape[0], :]], axis=0), at, MAIN)
        at += MAIN
    if pieces:
        product(pieces[0][...], at, pieces[0].shape[0])


def project_out(matrix, crops, rest):
    pieces = [p for crop in crops for p in crop] + ([rest] if rest is not None else [])
    length = MAIN * len(crops) + (rest.shape[0] if rest is not None else 0)
    width = matrix.shape[0]
    kernel = functools.partial(out_kernel, [len(crop) for crop in crops])
    return call(kernel, [(width // 4, length)] * 4, [matrix] + pieces)


def middle_kernel(*refs):
    term_refs, out_refs = refs[:-4], refs[-4:]
    step = out_refs[0].shape[0]
    at = 0
    for base in range(0, len(term_refs), 4):
        size = term_refs[base].shape[1]
        for k, out_ref in enumerate(out_refs):
            part = slice(k * step, (k + 1) * step)
            total = sum(ref[part, :].astype(F32) for ref in term_refs[base : base + 4])
            out_ref[:, at : at + size] = total.astype(BF16)
        at += size


def middle(groups):
    rows, length = groups[0][0].shape[0], sum(terms[0].shape[1] for terms in groups)
    return call(middle_kernel, [(rows // 4, length)] * 4, [term for terms in groups for term in terms])


def final_kernel(count, with_rest, *refs):
    terms, resid_refs, out_ref = refs[:4], refs[4:-1], refs[-1]

    def total(part):
        return terms[0][:, part].astype(F32) + terms[1][:, part].astype(F32) + terms[2][:, part].astype(F32) + terms[3][:, part].astype(F32)

    for k in range(count):
        part = slice(k * MAIN, (k + 1) * MAIN)
        out_ref[:, part] = (total(part) + resid_refs[k][:, :MAIN].astype(F32)).astype(BF16)
    if with_rest:
        part = slice(count * MAIN, count * MAIN + REST * len(resid_refs[count:]))
        rest = jnp.concatenate([ref[:, MAIN:].astype(F32) for ref in resid_refs[count:]], axis=1)
        out_ref[:, part] = (total(part) + rest).astype(BF16)


CHUNKS = ((0, 1, 2, 3, 6, 7), (4, 5))


def place_kernel(place_ref, *refs):
    out_ref, main_ref, rest_ref = refs[4:]
    count, thin, _ = out_ref.shape
    for d in range(2):
        parts = refs[2 * d : 2 * d + 2]
        for ref, blocks in zip(parts, CHUNKS):
            for k, r in enumerate(blocks):
                main_ref[count * d + r] = ref[:, k * MAIN : (k + 1) * MAIN].astype(F32)
        last = parts[1][:, 2 * MAIN :].astype(F32)
        for r in range(count):
            rest_ref[count * d + r] = jnp.broadcast_to(last[:, REST * r : REST * r + 1], (thin, 128))
    for slot in range(count):
        at = place_ref[slot]
        out_ref[slot, :, :MAIN] = main_ref[at].astype(BF16)
        out_ref[slot, :, MAIN:] = rest_ref[at][:, :1].astype(BF16)


def shards(crops_in, crop_table, ln_gain, w_qkv, q_gain, k_gain, w_up, b_up, w_out, w_down):
    _, tokens, model_width = crops_in.shape
    count_y = lax.axis_size("my")
    count_x = lax.axis_size("mx")
    at_y = lax.axis_index("my")
    at_m = lax.axis_index("mx")
    at_d = lax.axis_index("dp")
    width = model_width // count_y
    thin = width // count_x
    heads_local, head_dim = w_out.shape[0], w_out.shape[1]
    split_at = heads_local * head_dim
    hidden_width = w_up.shape[1]

    place_y = at_y.astype(jnp.int32).reshape(1)
    crop = crops_in[0]
    last = jnp.pad(crop[MAIN:].astype(F32), ((0, 7), (0, 0)))
    far_a, far_b = pack(place_y, crop, last, width, FIRST)
    barrier = lax.optimization_barrier
    far_a = swap(far_a, "my", 5)
    far_b = swap(far_b, "my", 4)

    matrix = jnp.concatenate([w_out.reshape(split_at, width).T, w_down.T], axis=1).reshape(count_x, thin, -1)
    near_a, back_a, near_b, back_b, beside, mine = pack(place_y, crop, last, width, SECOND)
    matrix, near_a, back_a, near_b, back_b, beside, mine = barrier((matrix, near_a, back_a, near_b, back_b, beside, mine))
    order = jnp.bitwise_xor(at_m, jnp.arange(count_x, dtype=jnp.int32))
    matrix = jnp.take(matrix, order, axis=0, mode="clip").reshape(width, -1)
    far_b, matrix, near_a, back_a, near_b, back_b = barrier((far_b, matrix, near_a, back_a, near_b, back_b))
    near_a, back_a = swap(near_a, "my", 3), swap(back_a, "my", 7)
    far_a, _, _ = barrier((far_a, near_a, back_a))
    near_a, back_a, near_b, back_b = barrier((near_a, back_a, swap(near_b, "my", 2), swap(back_b, "my", 6)))

    qkv_width = 3 * split_at
    weights_qkv = w_qkv.transpose(1, 2, 0, 3).reshape(3 * heads_local, width, head_dim)
    gain = ln_gain.astype(F32).reshape(1, width)
    resid = [None] * count_y
    place = at_m.astype(jnp.int32).reshape(1)

    def send(k, raw):
        other, resid[2 * k + 1] = call(
            send_kernel, [(ROWS, qkv_width + hidden_width), (thin, ROWS)], [place, raw, gain, weights_qkv, w_up], 1
        )
        return swap(other, "my", 1)

    def keep(k, raw, other):
        *terms, resid[2 * k] = call(
            keep_kernel,
            [(ROWS, qkv_width), (ROWS, hidden_width), (thin, ROWS)],
            [place, raw, gain, weights_qkv, w_up, other],
            1,
        )
        return terms

    def add(one, two):
        return call(add_kernel, [one.shape], [one, two])[0]

    far_other = send(2, far_a)
    far_parts = keep(2, far_b, far_other)
    far_qkv = swap(far_parts[0], "my", 2)
    far_up = swap(far_parts[1], "my", 6)
    beside, mine, _ = barrier((beside, mine, far_parts[0]))
    own_qkv, own_up = keep(0, mine, send(0, swap(beside, "my", 1)))
    near_a, back_a, _ = barrier((near_a, back_a, far_parts[0]))
    near_other = send(1, near_a)
    back_other = send(3, back_a)
    near_qkv, near_up = keep(1, near_b, near_other)
    near_qkv = swap(near_qkv, "my", 2)
    back_qkv, back_up = keep(3, back_b, back_other)
    back_qkv = swap(add(back_qkv, far_qkv), "my", 6)
    near_up, _ = barrier((add(near_up, far_up), near_qkv))
    near_up = swap(near_up, "my", 2)
    back_up, _ = barrier((back_up, back_qkv))
    back_up = swap(back_up, "my", 6)

    (attended,) = call(
        functools.partial(attend_kernel, tokens),
        [(ROWS, split_at)],
        [own_qkv, near_qkv, back_qkv, q_gain, k_gain],
    )
    (branch,) = call(
        hidden_kernel,
        [(ROWS, split_at + hidden_width)],
        [own_up, near_up, back_up, b_up.reshape(1, -1), attended],
    )

    cut = 128
    near_branch = swap(branch, "my", 2)
    back_branch = swap(branch, "my", 6)
    beside_branch = swap(branch, "my", 1)

    def spread(parts):
        return [parts[0]] + [swap(parts[k], "mx", 4 * k) for k in (1, 2, 3)]

    def output(blocks, groups, rest):
        parts = middle(groups)
        parts = [parts[0]] + [swap(parts[k], "mx", k) for k in (1, 2, 3)]
        base = [resid[r] for r in blocks] + (resid if rest else [])
        kernel = functools.partial(final_kernel, len(blocks), rest)
        (own,) = call(kernel, [parts[0].shape], list(parts) + base)
        return own, swap(own, "dp", 1)

    terms_0 = spread(project_out(matrix, [(branch,), (beside_branch,)], None))
    near_branch, back_branch, *terms_0 = barrier((near_branch, back_branch, *terms_0))
    far_lead = swap(back_branch[:cut], "my", 2)
    far_trail = swap(near_branch[cut:], "my", 6)
    near_side = swap(near_branch, "my", 1)
    back_side = swap(back_branch, "my", 1)
    parts = project_out(matrix, [(near_branch,), (near_side,), (back_branch,), (back_side,)], None)
    far_lead, far_trail, _ = barrier((far_lead, far_trail, parts[0]))
    own_0, other_0 = output(CHUNKS[0], [terms_0, spread(parts)], False)
    far_lead_side = swap(far_lead, "my", 1)
    far_trail_side = swap(far_trail, "my", 1)
    rest = jnp.concatenate(
        [
            piece[-REST:]
            for piece in (branch, beside_branch, near_branch, near_side, far_trail, far_trail_side, back_branch, back_side)
        ],
        axis=0,
    )
    parts = project_out(matrix, [(far_lead, far_trail), (far_lead_side, far_trail_side)], rest)
    own_1, other_1 = output(CHUNKS[1], [spread(parts)], True)

    chosen = lax.dynamic_slice_in_dim(crop_table, at_d * count_y, count_y)
    place = jnp.bitwise_xor(chosen // count_y, at_d) * count_y + jnp.bitwise_xor(chosen % count_y, at_y)
    result = pl.pallas_call(
        place_kernel,
        out_shape=jax.ShapeDtypeStruct((count_y, thin, tokens), BF16),
        in_specs=[SMEM] + [pl.BlockSpec(memory_space=pltpu.VMEM)] * 4,
        out_specs=pl.BlockSpec(memory_space=pltpu.VMEM),
        scratch_shapes=[pltpu.VMEM((2 * count_y, thin, MAIN), F32), pltpu.VMEM((2 * count_y, thin, 128), F32)],
        compiler_params=pltpu.CompilerParams(vmem_limit_bytes=LIMIT),
        cost_estimate=pl.CostEstimate(flops=1000, bytes_accessed=1000, transcendentals=0),
    )(place.astype(jnp.int32), own_0, own_1, other_0, other_1)
    return result.transpose(0, 2, 1)


def solution(mesh):
    placed = (
        P(("dp", "my"), None, None),
        P(),
        P("my"),
        P("my", "mx", None, None),
        P("mx", None),
        P("mx", None),
        P("my", "mx"),
        P("mx"),
        P("mx", None, "my"),
        P("mx", "my"),
    )
    return jax.shard_map(
        shards, mesh=mesh, in_specs=placed, out_specs=P("dp", None, ("my", "mx")), check_vma=False
    )
```

```python
import functools
import math

import jax
import jax.numpy as jnp
from jax import lax
from jax.experimental import pallas as pl
from jax.experimental.pallas import tpu as pltpu
from jax.sharding import PartitionSpec as P

D = 6144
EPS = 1e-06
F32 = jnp.float32
BF16 = jnp.bfloat16
MAIN = 256
REST = 16
ROWS = MAIN + REST
LANES = 384
FIRST = (5, 4)
HALF = 144
SECOND = (3, 7, 2, 6, 1, 0)
LIMIT = 16 * 1024 * 1024
SMEM = pl.BlockSpec(memory_space=pltpu.SMEM)


def swap(value, axis, mask):
    count = lax.axis_size(axis)
    return lax.ppermute(value, axis, [(a, a ^ mask) for a in range(count)])


def call(kernel, outs, args, scalars=0):
    return pl.pallas_call(
        kernel,
        out_shape=[jax.ShapeDtypeStruct(shape, BF16) for shape in outs],
        in_specs=[SMEM] * scalars + [pl.BlockSpec(memory_space=pltpu.VMEM)] * (len(args) - scalars),
        out_specs=[pl.BlockSpec(memory_space=pltpu.VMEM)] * len(outs),
        compiler_params=pltpu.CompilerParams(vmem_limit_bytes=LIMIT),
        cost_estimate=pl.CostEstimate(flops=1000, bytes_accessed=1000, transcendentals=0),
    )(*args)


def row_statistics(piece_of, count):
    first = second = 0.0
    for k in range(count):
        piece = piece_of(k)
        first = first + jnp.sum(piece, axis=1, keepdims=True)
        second = second + jnp.sum(piece * piece, axis=1, keepdims=True)
    mean = first / D
    return mean, lax.rsqrt(second / D - mean * mean + EPS)


def split_table(mean, scale):
    rows = mean.shape[0]
    lane = lax.broadcasted_iota(jnp.int32, (rows, 128), 1)
    table = jnp.zeros((rows, 128), F32)
    for k, value in ((1, mean), (4, scale)):
        for part in range(3):
            high = value.astype(BF16).astype(F32)
            table = jnp.where(lane == k + part, high, table)
            value = value - high
    return table


def pack_kernel(count, masks, at_ref, x_ref, crop_ref, last_ref, *out_refs):
    width = crop_ref.shape[1] // count
    table = split_table(
        *row_statistics(lambda k: crop_ref[:MAIN, k * width : (k + 1) * width].astype(F32), count)
    )
    final = split_table(*row_statistics(lambda k: last_ref[:, k * width : (k + 1) * width], count))
    final = jnp.where(lax.broadcasted_iota(jnp.int32, final.shape, 0) == 0, final, 0.0)
    table = jnp.concatenate([table, final, jnp.zeros((LANES - MAIN - final.shape[0], 128), F32)], axis=0)
    stats = jnp.transpose(table)[:REST]
    stats = jnp.concatenate([stats, jnp.zeros((REST, width - LANES), F32)], axis=1)
    row = lax.broadcasted_iota(jnp.int32, (REST, width), 0)
    at_y = at_ref[0]
    if masks == FIRST:
        for k in range(4):

            @pl.when(x_ref[0] == k)
            def _(k=k):
                start = pl.multiple_of(jnp.bitwise_xor(at_y, masks[k // 2]) * width, width)
                columns = pl.ds(start, width)
                if k % 2 == 0:
                    out_refs[0][...] = crop_ref[:HALF, columns]
                else:
                    out_refs[0][: MAIN + HALF - ROWS, :] = crop_ref[ROWS - HALF : MAIN, columns]
                    final = jnp.where(row == 0, last_ref[:1, columns], stats)
                    out_refs[0][MAIN + HALF - ROWS :, :] = final.astype(BF16)

        return
    for out_ref, mask in zip(out_refs, masks):
        columns = pl.ds(pl.multiple_of(jnp.bitwise_xor(at_y, mask) * width, width), width)
        out_ref[:MAIN, :] = crop_ref[:MAIN, columns]
        out_ref[MAIN:, :] = jnp.where(row == 0, last_ref[:1, columns], stats).astype(BF16)


def pack(at_y, at_x, crop, last, width, masks):
    kernel = functools.partial(pack_kernel, crop.shape[1] // width, masks)
    shapes = [(HALF, width)] if masks == FIRST else [(ROWS, width)] * len(masks)
    return call(kernel, shapes, [at_y, at_x, crop, last], 2)


def join_kernel(x_ref, *refs):
    pieces, out_refs = refs[:4], refs[4:]
    for x in range(4):

        @pl.when(x_ref[0] == x)
        def _(x=x):
            for k, out_ref in enumerate(out_refs):
                out_ref[:HALF, :] = pieces[(2 * k) ^ x][...]
                out_ref[HALF:, :] = pieces[(2 * k + 1) ^ x][2 * HALF - ROWS :, :]


def normalised(raw_ref, gain_ref):
    stats = raw_ref[MAIN:ROWS, :LANES].astype(F32)
    mean = (stats[1:2] + stats[2:3]) + stats[3:4]
    scale = (stats[4:5] + stats[5:6]) + stats[6:7]
    row = lax.broadcasted_iota(jnp.int32, (128, LANES), 0)
    table = jnp.where(row == 0, mean, jnp.where(row == 1, scale, 0.0))
    table = jnp.transpose(table)[:ROWS]
    return ((raw_ref[:ROWS, :].astype(F32) - table[:, :1]) * table[:, 1:2] * gain_ref[...]).astype(BF16)


def thin_columns(at_ref, raw_ref, thin_ref):
    rows, width = thin_ref.shape[0], raw_ref.shape[1]
    row = lax.broadcasted_iota(jnp.int32, (rows, width), 0)
    column = lax.broadcasted_iota(jnp.int32, (rows, width), 1)
    chosen = jnp.where(column == row + at_ref[0] * rows, 1.0, 0.0).astype(BF16)
    thin_ref[...] = lax.dot_general(
        chosen, raw_ref[:ROWS, :], (((1,), (1,)), ((), ())), preferred_element_type=F32
    ).astype(BF16)


def products(normed, qkv_ref, up_ref):
    blocks, _, size = qkv_ref.shape
    for k in range(0, blocks, 3):
        matrix = jnp.concatenate([qkv_ref[k], qkv_ref[k + 1], qkv_ref[k + 2]], axis=1)
        yield k * size, jnp.dot(normed, matrix, preferred_element_type=F32)
    for k in range(0, up_ref.shape[1], 768):
        yield blocks * size + k, jnp.dot(normed, up_ref[:, k : k + 768], preferred_element_type=F32)


def send_kernel(at_ref, raw_ref, gain_ref, qkv_ref, up_ref, out_ref, thin_ref):
    for at, value in products(normalised(raw_ref, gain_ref), qkv_ref, up_ref):
        out_ref[:, at : at + value.shape[1]] = value.astype(BF16)
    thin_columns(at_ref, raw_ref, thin_ref)


def keep_kernel(at_ref, raw_ref, gain_ref, qkv_ref, up_ref, other_ref, *refs):
    out_refs, thin_ref = list(refs[:-1]), refs[-1]
    base = 0
    for at, value in products(normalised(raw_ref, gain_ref), qkv_ref, up_ref):
        size = value.shape[1]
        if at - base == out_refs[0].shape[1]:
            base += out_refs.pop(0).shape[1]
        value = value + other_ref[:, at : at + size].astype(F32)
        out_refs[0][:, at - base : at - base + size] = value.astype(BF16)
    thin_columns(at_ref, raw_ref, thin_ref)


def add_kernel(one_ref, two_ref, out_ref):
    out_ref[...] = (one_ref[...].astype(F32) + two_ref[...].astype(F32)).astype(BF16)


def head_norm(entries, gain_row):
    center = entries - jnp.mean(entries, axis=-1, keepdims=True)
    spread = jnp.mean(center * center, axis=-1, keepdims=True)
    return (center * lax.rsqrt(spread + EPS) * gain_row).astype(BF16)


def attend_kernel(tokens, a_ref, b_ref, c_ref, q_gain_ref, k_gain_ref, out_ref):
    heads, width = q_gain_ref.shape
    live = lax.broadcasted_iota(jnp.int32, (ROWS, LANES), 1) < tokens
    spare = jnp.zeros((LANES - ROWS, width), BF16)

    def total(at):
        part = slice(at, at + width)
        return a_ref[:, part].astype(F32) + b_ref[:, part].astype(F32) + c_ref[:, part].astype(F32)

    for h in range(heads):
        at = 3 * width * h
        queries = head_norm(total(at), q_gain_ref[h : h + 1, :])
        key_rows = jnp.concatenate([head_norm(total(at + width), k_gain_ref[h : h + 1, :]), spare], axis=0)
        value_rows = jnp.concatenate([total(at + 2 * width).astype(BF16), spare], axis=0)
        scores = lax.dot_general(
            queries, key_rows, (((1,), (1,)), ((), ())), preferred_element_type=F32
        ) / math.sqrt(width)
        scores = jnp.where(live, scores, -1e30)
        weights = jnp.exp(scores - jnp.max(scores, axis=-1, keepdims=True))
        weights = weights / jnp.sum(weights, axis=-1, keepdims=True)
        out_ref[:, width * h : width * (h + 1)] = jnp.dot(
            weights.astype(BF16), value_rows, preferred_element_type=F32
        ).astype(BF16)


def hidden_kernel(a_ref, b_ref, c_ref, bias_ref, attended_ref, out_ref):
    at = attended_ref.shape[1]
    out_ref[:, :at] = attended_ref[...]
    for k in range(0, a_ref.shape[1], 256):
        part = slice(k, k + 256)
        value = a_ref[:, part].astype(F32) + b_ref[:, part].astype(F32) + c_ref[:, part].astype(F32)
        value = value + bias_ref[:, part]
        value = 0.5 * value * (1.0 + lax.erf(value * math.sqrt(0.5)))
        out_ref[:, at + k : at + k + 256] = value.astype(BF16)


def out_kernel(crops, matrix_ref, *refs):
    out_refs = refs[-4:]
    pieces = list(refs[:-4])
    step = matrix_ref.shape[0] // 4

    def product(rows, at, size):
        for k, out_ref in enumerate(out_refs):
            out_ref[:, at : at + size] = lax.dot_general(
                matrix_ref[k * step : (k + 1) * step, :], rows, (((1,), (1,)), ((), ())), preferred_element_type=F32
            ).astype(BF16)

    at = 0
    for parts in crops:
        rows = [pieces.pop(0) for _ in range(parts)]
        if parts == 1:
            product(rows[0][:MAIN, :], at, MAIN)
        else:
            product(jnp.concatenate([rows[0][...], rows[1][: MAIN - rows[0].shape[0], :]], axis=0), at, MAIN)
        at += MAIN
    if pieces:
        product(pieces[0][...], at, pieces[0].shape[0])


def project_out(matrix, crops, rest):
    pieces = [p for crop in crops for p in crop] + ([rest] if rest is not None else [])
    length = MAIN * len(crops) + (rest.shape[0] if rest is not None else 0)
    width = matrix.shape[0]
    kernel = functools.partial(out_kernel, [len(crop) for crop in crops])
    return call(kernel, [(width // 4, length)] * 4, [matrix] + pieces)


def middle_kernel(*refs):
    term_refs, out_refs = refs[:-4], refs[-4:]
    step = out_refs[0].shape[0]
    at = 0
    for base in range(0, len(term_refs), 4):
        size = term_refs[base].shape[1]
        for k, out_ref in enumerate(out_refs):
            part = slice(k * step, (k + 1) * step)
            total = sum(ref[part, :].astype(F32) for ref in term_refs[base : base + 4])
            out_ref[:, at : at + size] = total.astype(BF16)
        at += size


def middle(groups):
    rows, length = groups[0][0].shape[0], sum(terms[0].shape[1] for terms in groups)
    return call(middle_kernel, [(rows // 4, length)] * 4, [term for terms in groups for term in terms])


def final_kernel(count, with_rest, *refs):
    terms, resid_refs, out_ref = refs[:4], refs[4:-1], refs[-1]

    def total(part):
        return terms[0][:, part].astype(F32) + terms[1][:, part].astype(F32) + terms[2][:, part].astype(F32) + terms[3][:, part].astype(F32)

    for k in range(count):
        part = slice(k * MAIN, (k + 1) * MAIN)
        out_ref[:, part] = (total(part) + resid_refs[k][:, :MAIN].astype(F32)).astype(BF16)
    if with_rest:
        part = slice(count * MAIN, count * MAIN + REST * len(resid_refs[count:]))
        rest = jnp.concatenate([ref[:, MAIN:].astype(F32) for ref in resid_refs[count:]], axis=1)
        out_ref[:, part] = (total(part) + rest).astype(BF16)


CHUNKS = ((0, 1, 2, 3, 6, 7), (4, 5))


def place_kernel(place_ref, *refs):
    out_ref, main_ref, rest_ref = refs[4:]
    count, thin, _ = out_ref.shape
    for d in range(2):
        parts = refs[2 * d : 2 * d + 2]
        for ref, blocks in zip(parts, CHUNKS):
            for k, r in enumerate(blocks):
                main_ref[count * d + r] = ref[:, k * MAIN : (k + 1) * MAIN].astype(F32)
        last = parts[1][:, 2 * MAIN :].astype(F32)
        for r in range(count):
            rest_ref[count * d + r] = jnp.broadcast_to(last[:, REST * r : REST * r + 1], (thin, 128))
    for slot in range(count):
        at = place_ref[slot]
        out_ref[slot, :, :MAIN] = main_ref[at].astype(BF16)
        out_ref[slot, :, MAIN:] = rest_ref[at][:, :1].astype(BF16)


def shards(crops_in, crop_table, ln_gain, w_qkv, q_gain, k_gain, w_up, b_up, w_out, w_down):
    _, tokens, model_width = crops_in.shape
    count_y = lax.axis_size("my")
    count_x = lax.axis_size("mx")
    at_y = lax.axis_index("my")
    at_m = lax.axis_index("mx")
    at_d = lax.axis_index("dp")
    width = model_width // count_y
    thin = width // count_x
    heads_local, head_dim = w_out.shape[0], w_out.shape[1]
    split_at = heads_local * head_dim
    hidden_width = w_up.shape[1]

    place_y = at_y.astype(jnp.int32).reshape(1)
    crop = crops_in[0]
    last = jnp.pad(crop[MAIN:].astype(F32), ((0, 7), (0, 0)))
    place_x = (at_m // 4).astype(jnp.int32).reshape(1)
    barrier = lax.optimization_barrier

    (piece,) = pack(place_y, place_x, crop, last, width, FIRST)
    route = []
    for i in range(count_x):
        for j in range(count_y):
            route.append((i * count_y + j, i * count_y + (j ^ FIRST[i // 8])))
    piece = lax.ppermute(piece, ("mx", "my"), route)
    near_a, back_a, near_b, back_b, beside, mine = pack(place_y, place_x, crop, last, width, SECOND)
    piece, near_a, back_a, near_b, back_b = barrier((piece, near_a, back_a, near_b, back_b))
    pieces = [piece] + [swap(piece, "mx", 4 * k) for k in (1, 2, 3)]
    near_a, back_a = swap(near_a, "my", 3), swap(back_a, "my", 7)
    near_b, back_b = swap(near_b, "my", 2), swap(back_b, "my", 6)
    near_a, back_a, near_b, back_b, *pieces = barrier((near_a, back_a, near_b, back_b, *pieces))
    far_a, far_b = call(join_kernel, [(ROWS, width)] * 2, [place_x] + pieces, 1)

    qkv_width = 3 * split_at
    weights_qkv = w_qkv.transpose(1, 2, 0, 3).reshape(3 * heads_local, width, head_dim)
    gain = ln_gain.astype(F32).reshape(1, width)
    resid = [None] * count_y
    place = at_m.astype(jnp.int32).reshape(1)

    def send(k, raw):
        other, resid[2 * k + 1] = call(
            send_kernel, [(ROWS, qkv_width + hidden_width), (thin, ROWS)], [place, raw, gain, weights_qkv, w_up], 1
        )
        return swap(other, "my", 1)

    def keep(k, raw, other):
        *terms, resid[2 * k] = call(
            keep_kernel,
            [(ROWS, qkv_width), (ROWS, hidden_width), (thin, ROWS)],
            [place, raw, gain, weights_qkv, w_up, other],
            1,
        )
        return terms

    def add(one, two):
        return call(add_kernel, [one.shape], [one, two])[0]

    far_other = send(2, far_a)
    far_parts = keep(2, far_b, far_other)
    far_qkv = swap(far_parts[0], "my", 2)
    far_up = swap(far_parts[1], "my", 6)
    beside, mine, _ = barrier((beside, mine, far_parts[0]))
    own_qkv, own_up = keep(0, mine, send(0, swap(beside, "my", 1)))
    near_other = send(1, near_a)
    back_other = send(3, back_a)
    near_qkv, near_up = keep(1, near_b, near_other)
    near_qkv = swap(near_qkv, "my", 2)
    back_qkv, back_up = keep(3, back_b, back_other)
    back_qkv = swap(add(back_qkv, far_qkv), "my", 6)
    near_up = add(near_up, far_up)
    near_up_sent, _ = barrier((near_up, near_qkv))
    near_up_got = swap(near_up_sent, "my", 2)
    back_up, _ = barrier((back_up, back_qkv))
    back_up = swap(back_up, "my", 6)

    w_out, w_down, _ = barrier((w_out, w_down, near_up))
    matrix = jnp.concatenate([w_out.reshape(split_at, width).T, w_down.T], axis=1).reshape(count_x, thin, -1)
    order = jnp.bitwise_xor(at_m, jnp.arange(count_x, dtype=jnp.int32))
    matrix = jnp.take(matrix, order, axis=0, mode="clip").reshape(width, -1)
    matrix, near_qkv = barrier((matrix, near_qkv))

    (attended,) = call(
        functools.partial(attend_kernel, tokens),
        [(ROWS, split_at)],
        [own_qkv, near_qkv, back_qkv, q_gain, k_gain],
    )
    (branch,) = call(
        hidden_kernel,
        [(ROWS, split_at + hidden_width)],
        [own_up, near_up_got, back_up, b_up.reshape(1, -1), attended],
    )

    cut = 128
    near_branch = swap(branch, "my", 2)
    back_branch = swap(branch, "my", 6)
    beside_branch = swap(branch, "my", 1)

    def spread(parts):
        return [parts[0]] + [swap(parts[k], "mx", 4 * k) for k in (1, 2, 3)]

    def output(blocks, groups, rest):
        parts = middle(groups)
        parts = [parts[0]] + [swap(parts[k], "mx", k) for k in (1, 2, 3)]
        base = [resid[r] for r in blocks] + (resid if rest else [])
        kernel = functools.partial(final_kernel, len(blocks), rest)
        (own,) = call(kernel, [parts[0].shape], list(parts) + base)
        return own, swap(own, "dp", 1)

    terms_0 = spread(project_out(matrix, [(branch,), (beside_branch,)], None))
    near_branch, back_branch, *terms_0 = barrier((near_branch, back_branch, *terms_0))
    far_lead = swap(back_branch[:cut], "my", 2)
    far_trail = swap(near_branch[cut:], "my", 6)
    near_side = swap(near_branch, "my", 1)
    back_side = swap(back_branch, "my", 1)
    terms_1 = spread(project_out(matrix, [(near_branch,), (near_side,)], None))
    terms_2 = spread(project_out(matrix, [(back_branch,), (back_side,)], None))
    far_lead, far_trail, *terms_1 = barrier((far_lead, far_trail, *terms_1))
    own_0, other_0 = output(CHUNKS[0], [terms_0, terms_1, terms_2], False)
    far_lead_side = swap(far_lead, "my", 1)
    far_trail_side = swap(far_trail, "my", 1)
    rest = jnp.concatenate(
        [
            piece[-REST:]
            for piece in (branch, beside_branch, near_branch, near_side, far_trail, far_trail_side, back_branch, back_side)
        ],
        axis=0,
    )
    parts = project_out(matrix, [(far_lead, far_trail), (far_lead_side, far_trail_side)], rest)
    own_1, other_1 = output(CHUNKS[1], [spread(parts)], True)

    chosen = lax.dynamic_slice_in_dim(crop_table, at_d * count_y, count_y)
    place = jnp.bitwise_xor(chosen // count_y, at_d) * count_y + jnp.bitwise_xor(chosen % count_y, at_y)
    result = pl.pallas_call(
        place_kernel,
        out_shape=jax.ShapeDtypeStruct((count_y, thin, tokens), BF16),
        in_specs=[SMEM] + [pl.BlockSpec(memory_space=pltpu.VMEM)] * 4,
        out_specs=pl.BlockSpec(memory_space=pltpu.VMEM),
        scratch_shapes=[pltpu.VMEM((2 * count_y, thin, MAIN), F32), pltpu.VMEM((2 * count_y, thin, 128), F32)],
        compiler_params=pltpu.CompilerParams(vmem_limit_bytes=LIMIT),
        cost_estimate=pl.CostEstimate(flops=1000, bytes_accessed=1000, transcendentals=0),
    )(place.astype(jnp.int32), own_0, own_1, other_0, other_1)
    return result.transpose(0, 2, 1)


def solution(mesh):
    placed = (
        P(("dp", "my"), None, None),
        P(),
        P("my"),
        P("my", "mx", None, None),
        P("mx", None),
        P("mx", None),
        P("my", "mx"),
        P("mx"),
        P("mx", None, "my"),
        P("mx", "my"),
    )
    return jax.shard_map(
        shards, mesh=mesh, in_specs=placed, out_specs=P("dp", None, ("my", "mx")), check_vma=False
    )
```

```python
import functools
import math

import jax
import jax.numpy as jnp
from jax import lax
from jax.experimental import pallas as pl
from jax.experimental.pallas import tpu as pltpu
from jax.sharding import PartitionSpec as P

D = 6144
EPS = 1e-06
F32 = jnp.float32
BF16 = jnp.bfloat16
MAIN = 256
REST = 16
ROWS = MAIN + REST
LANES = 384
FIRST = (5, 4)
HALF = 144
SECOND = (3, 7, 2, 6, 1, 0)
LIMIT = 16 * 1024 * 1024
SMEM = pl.BlockSpec(memory_space=pltpu.SMEM)


def swap(value, axis, mask):
    count = lax.axis_size(axis)
    return lax.ppermute(value, axis, [(a, a ^ mask) for a in range(count)])


def call(kernel, outs, args, scalars=0):
    return pl.pallas_call(
        kernel,
        out_shape=[jax.ShapeDtypeStruct(shape, BF16) for shape in outs],
        in_specs=[SMEM] * scalars + [pl.BlockSpec(memory_space=pltpu.VMEM)] * (len(args) - scalars),
        out_specs=[pl.BlockSpec(memory_space=pltpu.VMEM)] * len(outs),
        compiler_params=pltpu.CompilerParams(vmem_limit_bytes=LIMIT),
        cost_estimate=pl.CostEstimate(flops=1000, bytes_accessed=1000, transcendentals=0),
    )(*args)


def row_statistics(piece_of, count):
    first = second = 0.0
    for k in range(count):
        piece = piece_of(k)
        first = first + jnp.sum(piece, axis=1, keepdims=True)
        second = second + jnp.sum(piece * piece, axis=1, keepdims=True)
    mean = first / D
    return mean, lax.rsqrt(second / D - mean * mean + EPS)


def split_table(mean, scale):
    rows = mean.shape[0]
    lane = lax.broadcasted_iota(jnp.int32, (rows, 128), 1)
    table = jnp.zeros((rows, 128), F32)
    for k, value in ((1, mean), (4, scale)):
        for part in range(3):
            high = value.astype(BF16).astype(F32)
            table = jnp.where(lane == k + part, high, table)
            value = value - high
    return table


def pack_kernel(count, masks, at_ref, x_ref, crop_ref, last_ref, *out_refs):
    width = crop_ref.shape[1] // count
    table = split_table(
        *row_statistics(lambda k: crop_ref[:MAIN, k * width : (k + 1) * width].astype(F32), count)
    )
    final = split_table(*row_statistics(lambda k: last_ref[:, k * width : (k + 1) * width], count))
    final = jnp.where(lax.broadcasted_iota(jnp.int32, final.shape, 0) == 0, final, 0.0)
    table = jnp.concatenate([table, final, jnp.zeros((LANES - MAIN - final.shape[0], 128), F32)], axis=0)
    stats = jnp.transpose(table)[:REST]
    stats = jnp.concatenate([stats, jnp.zeros((REST, width - LANES), F32)], axis=1)
    row = lax.broadcasted_iota(jnp.int32, (REST, width), 0)
    at_y = at_ref[0]
    if masks == FIRST:
        for k in range(4):

            @pl.when(x_ref[0] == k)
            def _(k=k):
                start = pl.multiple_of(jnp.bitwise_xor(at_y, masks[k // 2]) * width, width)
                columns = pl.ds(start, width)
                if k % 2 == 0:
                    out_refs[0][...] = crop_ref[:HALF, columns]
                else:
                    out_refs[0][: MAIN + HALF - ROWS, :] = crop_ref[ROWS - HALF : MAIN, columns]
                    final = jnp.where(row == 0, last_ref[:1, columns], stats)
                    out_refs[0][MAIN + HALF - ROWS :, :] = final.astype(BF16)

        return
    for out_ref, mask in zip(out_refs, masks):
        columns = pl.ds(pl.multiple_of(jnp.bitwise_xor(at_y, mask) * width, width), width)
        out_ref[:MAIN, :] = crop_ref[:MAIN, columns]
        out_ref[MAIN:, :] = jnp.where(row == 0, last_ref[:1, columns], stats).astype(BF16)


def pack(at_y, at_x, crop, last, width, masks):
    kernel = functools.partial(pack_kernel, crop.shape[1] // width, masks)
    shapes = [(HALF, width)] if masks == FIRST else [(ROWS, width)] * len(masks)
    return call(kernel, shapes, [at_y, at_x, crop, last], 2)


def join_kernel(x_ref, *refs):
    pieces, out_refs = refs[:4], refs[4:]
    for x in range(4):

        @pl.when(x_ref[0] == x)
        def _(x=x):
            for k, out_ref in enumerate(out_refs):
                out_ref[:HALF, :] = pieces[(2 * k) ^ x][...]
                out_ref[HALF:, :] = pieces[(2 * k + 1) ^ x][2 * HALF - ROWS :, :]


def normalised(raw_ref, gain_ref):
    stats = raw_ref[MAIN:ROWS, :LANES].astype(F32)
    mean = (stats[1:2] + stats[2:3]) + stats[3:4]
    scale = (stats[4:5] + stats[5:6]) + stats[6:7]
    row = lax.broadcasted_iota(jnp.int32, (128, LANES), 0)
    table = jnp.where(row == 0, mean, jnp.where(row == 1, scale, 0.0))
    table = jnp.transpose(table)[:ROWS]
    return ((raw_ref[:ROWS, :].astype(F32) - table[:, :1]) * table[:, 1:2] * gain_ref[...]).astype(BF16)


def thin_columns(at_ref, raw_ref, thin_ref):
    rows, width = thin_ref.shape[0], raw_ref.shape[1]
    row = lax.broadcasted_iota(jnp.int32, (rows, width), 0)
    column = lax.broadcasted_iota(jnp.int32, (rows, width), 1)
    chosen = jnp.where(column == row + at_ref[0] * rows, 1.0, 0.0).astype(BF16)
    thin_ref[...] = lax.dot_general(
        chosen, raw_ref[:ROWS, :], (((1,), (1,)), ((), ())), preferred_element_type=F32
    ).astype(BF16)


def products(normed, qkv_ref, up_ref):
    blocks, _, size = qkv_ref.shape
    for k in range(0, blocks, 3):
        matrix = jnp.concatenate([qkv_ref[k], qkv_ref[k + 1], qkv_ref[k + 2]], axis=1)
        yield k * size, jnp.dot(normed, matrix, preferred_element_type=F32)
    for k in range(0, up_ref.shape[1], 768):
        yield blocks * size + k, jnp.dot(normed, up_ref[:, k : k + 768], preferred_element_type=F32)


def send_kernel(at_ref, raw_ref, gain_ref, qkv_ref, up_ref, out_ref, thin_ref):
    for at, value in products(normalised(raw_ref, gain_ref), qkv_ref, up_ref):
        out_ref[:, at : at + value.shape[1]] = value.astype(BF16)
    thin_columns(at_ref, raw_ref, thin_ref)


def keep_kernel(at_ref, raw_ref, gain_ref, qkv_ref, up_ref, other_ref, *refs):
    out_refs, thin_ref = list(refs[:-1]), refs[-1]
    base = 0
    for at, value in products(normalised(raw_ref, gain_ref), qkv_ref, up_ref):
        size = value.shape[1]
        if at - base == out_refs[0].shape[1]:
            base += out_refs.pop(0).shape[1]
        value = value + other_ref[:, at : at + size].astype(F32)
        out_refs[0][:, at - base : at - base + size] = value.astype(BF16)
    thin_columns(at_ref, raw_ref, thin_ref)


def add_kernel(one_ref, two_ref, out_ref):
    out_ref[...] = (one_ref[...].astype(F32) + two_ref[...].astype(F32)).astype(BF16)


def head_norm(entries, gain_row):
    center = entries - jnp.mean(entries, axis=-1, keepdims=True)
    spread = jnp.mean(center * center, axis=-1, keepdims=True)
    return (center * lax.rsqrt(spread + EPS) * gain_row).astype(BF16)


def attend_kernel(tokens, a_ref, b_ref, c_ref, q_gain_ref, k_gain_ref, out_ref):
    heads, width = q_gain_ref.shape
    live = lax.broadcasted_iota(jnp.int32, (ROWS, LANES), 1) < tokens
    spare = jnp.zeros((LANES - ROWS, width), BF16)

    def total(at):
        part = slice(at, at + width)
        return a_ref[:, part].astype(F32) + b_ref[:, part].astype(F32) + c_ref[:, part].astype(F32)

    for h in range(heads):
        at = 3 * width * h
        queries = head_norm(total(at), q_gain_ref[h : h + 1, :])
        key_rows = jnp.concatenate([head_norm(total(at + width), k_gain_ref[h : h + 1, :]), spare], axis=0)
        value_rows = jnp.concatenate([total(at + 2 * width).astype(BF16), spare], axis=0)
        scores = lax.dot_general(
            queries, key_rows, (((1,), (1,)), ((), ())), preferred_element_type=F32
        ) / math.sqrt(width)
        scores = jnp.where(live, scores, -1e30)
        weights = jnp.exp(scores - jnp.max(scores, axis=-1, keepdims=True))
        weights = weights / jnp.sum(weights, axis=-1, keepdims=True)
        out_ref[:, width * h : width * (h + 1)] = jnp.dot(
            weights.astype(BF16), value_rows, preferred_element_type=F32
        ).astype(BF16)


def hidden_kernel(a_ref, b_ref, c_ref, bias_ref, attended_ref, out_ref):
    at = attended_ref.shape[1]
    out_ref[:, :at] = attended_ref[...]
    for k in range(0, a_ref.shape[1], 256):
        part = slice(k, k + 256)
        value = a_ref[:, part].astype(F32) + b_ref[:, part].astype(F32) + c_ref[:, part].astype(F32)
        value = value + bias_ref[:, part]
        value = 0.5 * value * (1.0 + lax.erf(value * math.sqrt(0.5)))
        out_ref[:, at + k : at + k + 256] = value.astype(BF16)


def out_kernel(crops, before, matrix_ref, *refs):
    out_refs = refs[-4:]
    pieces = list(refs[before:-4])
    step = matrix_ref.shape[0] // 4

    def product(rows, at, size):
        for k, out_ref in enumerate(out_refs):
            out_ref[:, at : at + size] = lax.dot_general(
                matrix_ref[k * step : (k + 1) * step, :], rows, (((1,), (1,)), ((), ())), preferred_element_type=F32
            ).astype(BF16)

    at = 0
    for ref, out_ref in zip(refs[:before], out_refs):
        at = ref.shape[1]
        out_ref[:, :at] = ref[...]
    for parts in crops:
        rows = [pieces.pop(0) for _ in range(parts)]
        if parts == 1:
            product(rows[0][:MAIN, :], at, MAIN)
        else:
            product(jnp.concatenate([rows[0][...], rows[1][: MAIN - rows[0].shape[0], :]], axis=0), at, MAIN)
        at += MAIN
    if pieces:
        product(pieces[0][...], at, pieces[0].shape[0])


def project_out(matrix, crops, rest=None, before=()):
    pieces = [p for crop in crops for p in crop] + ([rest] if rest is not None else [])
    length = MAIN * len(crops) + (rest.shape[0] if rest is not None else 0)
    width = matrix.shape[0]
    length += before[0].shape[1] if before else 0
    kernel = functools.partial(out_kernel, [len(crop) for crop in crops], len(before))
    return call(kernel, [(width // 4, length)] * 4, [matrix] + list(before) + pieces)


def middle_kernel(*refs):
    term_refs, out_refs = refs[:-4], refs[-4:]
    step = out_refs[0].shape[0]
    at = 0
    for base in range(0, len(term_refs), 4):
        size = term_refs[base].shape[1]
        for k, out_ref in enumerate(out_refs):
            part = slice(k * step, (k + 1) * step)
            total = sum(ref[part, :].astype(F32) for ref in term_refs[base : base + 4])
            out_ref[:, at : at + size] = total.astype(BF16)
        at += size


def middle(groups):
    rows, length = groups[0][0].shape[0], sum(terms[0].shape[1] for terms in groups)
    return call(middle_kernel, [(rows // 4, length)] * 4, [term for terms in groups for term in terms])


def final_kernel(count, with_rest, *refs):
    terms, resid_refs, out_ref = refs[:4], refs[4:-1], refs[-1]

    def total(part):
        return terms[0][:, part].astype(F32) + terms[1][:, part].astype(F32) + terms[2][:, part].astype(F32) + terms[3][:, part].astype(F32)

    for k in range(count):
        part = slice(k * MAIN, (k + 1) * MAIN)
        out_ref[:, part] = (total(part) + resid_refs[k][:, :MAIN].astype(F32)).astype(BF16)
    if with_rest:
        part = slice(count * MAIN, count * MAIN + REST * len(resid_refs[count:]))
        rest = jnp.concatenate([ref[:, MAIN:].astype(F32) for ref in resid_refs[count:]], axis=1)
        out_ref[:, part] = (total(part) + rest).astype(BF16)


CHUNKS = ((0, 1, 2, 3), (6, 7, 4, 5))


def place_kernel(place_ref, *refs):
    out_ref, main_ref, rest_ref = refs[4:]
    count, thin, _ = out_ref.shape
    for d in range(2):
        parts = refs[2 * d : 2 * d + 2]
        for ref, blocks in zip(parts, CHUNKS):
            for k, r in enumerate(blocks):
                main_ref[count * d + r] = ref[:, k * MAIN : (k + 1) * MAIN].astype(F32)
        last = parts[1][:, len(CHUNKS[1]) * MAIN :].astype(F32)
        for r in range(count):
            rest_ref[count * d + r] = jnp.broadcast_to(last[:, REST * r : REST * r + 1], (thin, 128))
    for slot in range(count):
        at = place_ref[slot]
        out_ref[slot, :, :MAIN] = main_ref[at].astype(BF16)
        out_ref[slot, :, MAIN:] = rest_ref[at][:, :1].astype(BF16)


def shards(crops_in, crop_table, ln_gain, w_qkv, q_gain, k_gain, w_up, b_up, w_out, w_down):
    _, tokens, model_width = crops_in.shape
    count_y = lax.axis_size("my")
    count_x = lax.axis_size("mx")
    at_y = lax.axis_index("my")
    at_m = lax.axis_index("mx")
    at_d = lax.axis_index("dp")
    width = model_width // count_y
    thin = width // count_x
    heads_local, head_dim = w_out.shape[0], w_out.shape[1]
    split_at = heads_local * head_dim
    hidden_width = w_up.shape[1]

    place_y = at_y.astype(jnp.int32).reshape(1)
    crop = crops_in[0]
    last = jnp.pad(crop[MAIN:].astype(F32), ((0, 7), (0, 0)))
    place_x = (at_m // 4).astype(jnp.int32).reshape(1)
    barrier = lax.optimization_barrier

    (piece,) = pack(place_y, place_x, crop, last, width, FIRST)
    route = []
    for i in range(count_x):
        for j in range(count_y):
            route.append((i * count_y + j, i * count_y + (j ^ FIRST[i // 8])))
    piece = lax.ppermute(piece, ("mx", "my"), route)
    near_a, back_a, near_b, back_b, beside, mine = pack(place_y, place_x, crop, last, width, SECOND)
    near_a, back_a = barrier((swap(near_a, "my", 3), swap(back_a, "my", 7)))
    near_b, back_b, _, _ = barrier((near_b, back_b, near_a, back_a))
    near_b, back_b = swap(near_b, "my", 2), swap(back_b, "my", 6)
    pieces = [piece] + [swap(piece, "mx", 4 * k) for k in (1, 2, 3)]
    near_a, back_a, near_b, back_b, *pieces = barrier((near_a, back_a, near_b, back_b, *pieces))
    far_a, far_b = call(join_kernel, [(ROWS, width)] * 2, [place_x] + pieces, 1)

    qkv_width = 3 * split_at
    weights_qkv = w_qkv.transpose(1, 2, 0, 3).reshape(3 * heads_local, width, head_dim)
    gain = ln_gain.astype(F32).reshape(1, width)
    resid = [None] * count_y
    place = at_m.astype(jnp.int32).reshape(1)

    def send(k, raw):
        other, resid[2 * k + 1] = call(
            send_kernel, [(ROWS, qkv_width + hidden_width), (thin, ROWS)], [place, raw, gain, weights_qkv, w_up], 1
        )
        return swap(other, "my", 1)

    def keep(k, raw, other):
        *terms, resid[2 * k] = call(
            keep_kernel,
            [(ROWS, qkv_width), (ROWS, hidden_width), (thin, ROWS)],
            [place, raw, gain, weights_qkv, w_up, other],
            1,
        )
        return terms

    def add(one, two):
        return call(add_kernel, [one.shape], [one, two])[0]

    far_other = send(2, far_a)
    far_parts = keep(2, far_b, far_other)
    far_qkv = swap(far_parts[0], "my", 2)
    far_up = swap(far_parts[1], "my", 6)
    beside, mine, _ = barrier((beside, mine, far_parts[0]))
    own_qkv, own_up = keep(0, mine, send(0, swap(beside, "my", 1)))
    near_other = send(1, near_a)
    back_other = send(3, back_a)
    near_qkv, near_up = keep(1, near_b, near_other)
    near_qkv = swap(near_qkv, "my", 2)
    back_qkv, back_up = keep(3, back_b, back_other)
    back_qkv = swap(add(back_qkv, far_qkv), "my", 6)
    near_up = add(near_up, far_up)
    near_up_sent, _ = barrier((near_up, near_qkv))
    near_up_got = swap(near_up_sent, "my", 2)
    back_up, _ = barrier((back_up, back_qkv))
    back_up = swap(back_up, "my", 6)

    w_out, w_down, _ = barrier((w_out, w_down, near_up))
    matrix = jnp.concatenate([w_out.reshape(split_at, width).T, w_down.T], axis=1).reshape(count_x, thin, -1)
    order = jnp.bitwise_xor(at_m, jnp.arange(count_x, dtype=jnp.int32))
    matrix = jnp.take(matrix, order, axis=0, mode="clip").reshape(width, -1)
    matrix, near_qkv = barrier((matrix, near_qkv))

    (attended,) = call(
        functools.partial(attend_kernel, tokens),
        [(ROWS, split_at)],
        [own_qkv, near_qkv, back_qkv, q_gain, k_gain],
    )
    (branch,) = call(
        hidden_kernel,
        [(ROWS, split_at + hidden_width)],
        [own_up, near_up_got, back_up, b_up.reshape(1, -1), attended],
    )

    cut = 128
    near_branch = swap(branch, "my", 2)
    back_branch = swap(branch, "my", 6)
    beside_branch = swap(branch, "my", 1)

    def spread(parts):
        return [parts[0]] + [swap(parts[k], "mx", 4 * k) for k in (1, 2, 3)]

    def output(blocks, groups, rest):
        parts = middle(groups)
        parts = [parts[0]] + [swap(parts[k], "mx", k) for k in (1, 2, 3)]
        base = [resid[r] for r in blocks] + (resid if rest else [])
        kernel = functools.partial(final_kernel, len(blocks), rest)
        (own,) = call(kernel, [parts[0].shape], list(parts) + base)
        return own, swap(own, "dp", 1)

    terms_0 = spread(project_out(matrix, [(branch,), (beside_branch,)]))
    near_branch, back_branch, *terms_0 = barrier((near_branch, back_branch, *terms_0))
    far_lead = swap(back_branch[:cut], "my", 2)
    far_trail = swap(near_branch[cut:], "my", 6)
    near_side = swap(near_branch, "my", 1)
    back_side = swap(back_branch, "my", 1)
    terms_1 = spread(project_out(matrix, [(near_branch,), (near_side,)]))
    before = project_out(matrix, [(back_branch,), (back_side,)])
    far_lead, far_trail, *before = barrier((far_lead, far_trail, *before))
    far_lead, far_trail, *terms_1 = barrier((far_lead, far_trail, *terms_1))
    own_0, other_0 = output(CHUNKS[0], [terms_0, terms_1], False)
    far_lead_side = swap(far_lead, "my", 1)
    far_trail_side = swap(far_trail, "my", 1)
    rest = jnp.concatenate(
        [
            piece[-REST:]
            for piece in (branch, beside_branch, near_branch, near_side, far_trail, far_trail_side, back_branch, back_side)
        ],
        axis=0,
    )
    parts = project_out(matrix, [(far_lead, far_trail), (far_lead_side, far_trail_side)], rest, before)
    terms = spread(parts)
    own_0, *terms = barrier((own_0, *terms))
    own_1, other_1 = output(CHUNKS[1], [terms], True)

    chosen = lax.dynamic_slice_in_dim(crop_table, at_d * count_y, count_y)
    place = jnp.bitwise_xor(chosen // count_y, at_d) * count_y + jnp.bitwise_xor(chosen % count_y, at_y)
    result = pl.pallas_call(
        place_kernel,
        out_shape=jax.ShapeDtypeStruct((count_y, thin, tokens), BF16),
        in_specs=[SMEM] + [pl.BlockSpec(memory_space=pltpu.VMEM)] * 4,
        out_specs=pl.BlockSpec(memory_space=pltpu.VMEM),
        scratch_shapes=[pltpu.VMEM((2 * count_y, thin, MAIN), F32), pltpu.VMEM((2 * count_y, thin, 128), F32)],
        compiler_params=pltpu.CompilerParams(vmem_limit_bytes=LIMIT),
        cost_estimate=pl.CostEstimate(flops=1000, bytes_accessed=1000, transcendentals=0),
    )(place.astype(jnp.int32), own_0, own_1, other_0, other_1)
    return result.transpose(0, 2, 1)


def solution(mesh):
    placed = (
        P(("dp", "my"), None, None),
        P(),
        P("my"),
        P("my", "mx", None, None),
        P("mx", None),
        P("mx", None),
        P("my", "mx"),
        P("mx"),
        P("mx", None, "my"),
        P("mx", "my"),
    )
    return jax.shard_map(
        shards, mesh=mesh, in_specs=placed, out_specs=P("dp", None, ("my", "mx")), check_vma=False
    )
```

```python
import functools
import math

import jax
import jax.numpy as jnp
from jax import lax
from jax.experimental import pallas as pl
from jax.experimental.pallas import tpu as pltpu
from jax.sharding import PartitionSpec as P

D = 6144
EPS = 1e-06
F32 = jnp.float32
BF16 = jnp.bfloat16
MAIN = 256
REST = 16
ROWS = MAIN + REST
LANES = 384
FIRST = (5, 4)
HALF = 144
SECOND = (3, 7, 2, 6, 1, 0)
LIMIT = 16 * 1024 * 1024
SMEM = pl.BlockSpec(memory_space=pltpu.SMEM)


def swap(value, axis, mask):
    count = lax.axis_size(axis)
    return lax.ppermute(value, axis, [(a, a ^ mask) for a in range(count)])


def sent(parts, step):
    got = list(parts)
    for k in (1, 3, 2):
        got[k] = swap(parts[k], "mx", k * step)
    return got


def call(kernel, outs, args, scalars=0, size=1000):
    return pl.pallas_call(
        kernel,
        out_shape=[jax.ShapeDtypeStruct(shape, BF16) for shape in outs],
        in_specs=[SMEM] * scalars + [pl.BlockSpec(memory_space=pltpu.VMEM)] * (len(args) - scalars),
        out_specs=[pl.BlockSpec(memory_space=pltpu.VMEM)] * len(outs),
        compiler_params=pltpu.CompilerParams(vmem_limit_bytes=LIMIT),
        cost_estimate=pl.CostEstimate(flops=1000, bytes_accessed=size, transcendentals=0),
    )(*args)


def row_statistics(piece_of, count):
    first = second = 0.0
    for k in range(count):
        piece = piece_of(k)
        first = first + jnp.sum(piece, axis=1, keepdims=True)
        second = second + jnp.sum(piece * piece, axis=1, keepdims=True)
    mean = first / D
    return mean, lax.rsqrt(second / D - mean * mean + EPS)


def split_table(mean, scale):
    rows = mean.shape[0]
    lane = lax.broadcasted_iota(jnp.int32, (rows, 128), 1)
    table = jnp.zeros((rows, 128), F32)
    for k, value in ((1, mean), (4, scale)):
        for part in range(3):
            high = value.astype(BF16).astype(F32)
            table = jnp.where(lane == k + part, high, table)
            value = value - high
    return table


def pack_kernel(count, masks, at_ref, x_ref, crop_ref, last_ref, *out_refs):
    width = crop_ref.shape[1] // count
    table = split_table(
        *row_statistics(lambda k: crop_ref[:MAIN, k * width : (k + 1) * width].astype(F32), count)
    )
    final = split_table(*row_statistics(lambda k: last_ref[:, k * width : (k + 1) * width], count))
    final = jnp.where(lax.broadcasted_iota(jnp.int32, final.shape, 0) == 0, final, 0.0)
    table = jnp.concatenate([table, final, jnp.zeros((LANES - MAIN - final.shape[0], 128), F32)], axis=0)
    stats = jnp.transpose(table)[:REST]
    stats = jnp.concatenate([stats, jnp.zeros((REST, width - LANES), F32)], axis=1)
    row = lax.broadcasted_iota(jnp.int32, (REST, width), 0)
    at_y = at_ref[0]
    if masks == FIRST:
        for k in range(4):

            @pl.when(x_ref[0] == k)
            def _(k=k):
                start = pl.multiple_of(jnp.bitwise_xor(at_y, masks[k // 2]) * width, width)
                columns = pl.ds(start, width)
                if k % 2 == 0:
                    out_refs[0][...] = crop_ref[:HALF, columns]
                else:
                    out_refs[0][: MAIN + HALF - ROWS, :] = crop_ref[ROWS - HALF : MAIN, columns]
                    final = jnp.where(row == 0, last_ref[:1, columns], stats)
                    out_refs[0][MAIN + HALF - ROWS :, :] = final.astype(BF16)

        return
    for out_ref, mask in zip(out_refs, masks):
        columns = pl.ds(pl.multiple_of(jnp.bitwise_xor(at_y, mask) * width, width), width)
        out_ref[:MAIN, :] = crop_ref[:MAIN, columns]
        out_ref[MAIN:, :] = jnp.where(row == 0, last_ref[:1, columns], stats).astype(BF16)


def pack(at_y, at_x, crop, last, width, masks):
    kernel = functools.partial(pack_kernel, crop.shape[1] // width, masks)
    shapes = [(HALF, width)] if masks == FIRST else [(ROWS, width)] * len(masks)
    return call(kernel, shapes, [at_y, at_x, crop, last], 2)


def join_kernel(x_ref, *refs):
    pieces, out_refs = refs[:4], refs[4:]
    for x in range(4):

        @pl.when(x_ref[0] == x)
        def _(x=x):
            for k, out_ref in enumerate(out_refs):
                out_ref[:HALF, :] = pieces[(2 * k) ^ x][...]
                out_ref[HALF:, :] = pieces[(2 * k + 1) ^ x][2 * HALF - ROWS :, :]


def normalised(raw_ref, gain_ref):
    stats = raw_ref[MAIN:ROWS, :LANES].astype(F32)
    mean = (stats[1:2] + stats[2:3]) + stats[3:4]
    scale = (stats[4:5] + stats[5:6]) + stats[6:7]
    row = lax.broadcasted_iota(jnp.int32, (128, LANES), 0)
    table = jnp.where(row == 0, mean, jnp.where(row == 1, scale, 0.0))
    table = jnp.transpose(table)[:ROWS]
    return ((raw_ref[:ROWS, :].astype(F32) - table[:, :1]) * table[:, 1:2] * gain_ref[...]).astype(BF16)


def thin_columns(at_ref, raw_ref, thin_ref):
    rows, width = thin_ref.shape[0], raw_ref.shape[1]
    row = lax.broadcasted_iota(jnp.int32, (rows, width), 0)
    column = lax.broadcasted_iota(jnp.int32, (rows, width), 1)
    chosen = jnp.where(column == row + at_ref[0] * rows, 1.0, 0.0).astype(BF16)
    thin_ref[...] = lax.dot_general(
        chosen, raw_ref[:ROWS, :], (((1,), (1,)), ((), ())), preferred_element_type=F32
    ).astype(BF16)


def products(normed, qkv_ref, up_ref):
    blocks, _, size = qkv_ref.shape
    for k in range(0, blocks, 3):
        matrix = jnp.concatenate([qkv_ref[k], qkv_ref[k + 1], qkv_ref[k + 2]], axis=1)
        yield k * size, jnp.dot(normed, matrix, preferred_element_type=F32)
    for k in range(0, up_ref.shape[1], 768):
        yield blocks * size + k, jnp.dot(normed, up_ref[:, k : k + 768], preferred_element_type=F32)


def send_kernel(at_ref, raw_ref, gain_ref, qkv_ref, up_ref, out_ref, thin_ref):
    for at, value in products(normalised(raw_ref, gain_ref), qkv_ref, up_ref):
        out_ref[:, at : at + value.shape[1]] = value.astype(BF16)
    thin_columns(at_ref, raw_ref, thin_ref)


def keep_kernel(at_ref, raw_ref, gain_ref, qkv_ref, up_ref, other_ref, *refs):
    out_refs, thin_ref = list(refs[:-1]), refs[-1]
    base = 0
    for at, value in products(normalised(raw_ref, gain_ref), qkv_ref, up_ref):
        size = value.shape[1]
        if at - base == out_refs[0].shape[1]:
            base += out_refs.pop(0).shape[1]
        value = value + other_ref[:, at : at + size].astype(F32)
        out_refs[0][:, at - base : at - base + size] = value.astype(BF16)
    thin_columns(at_ref, raw_ref, thin_ref)


def add_kernel(one_ref, two_ref, out_ref):
    out_ref[...] = (one_ref[...].astype(F32) + two_ref[...].astype(F32)).astype(BF16)


def head_norm(entries, gain_row):
    center = entries - jnp.mean(entries, axis=-1, keepdims=True)
    spread = jnp.mean(center * center, axis=-1, keepdims=True)
    return (center * lax.rsqrt(spread + EPS) * gain_row).astype(BF16)


def attend_kernel(tokens, a_ref, b_ref, c_ref, q_gain_ref, k_gain_ref, out_ref):
    heads, width = q_gain_ref.shape
    live = lax.broadcasted_iota(jnp.int32, (ROWS, LANES), 1) < tokens
    spare = jnp.zeros((LANES - ROWS, width), BF16)

    def total(at):
        part = slice(at, at + width)
        return a_ref[:, part].astype(F32) + b_ref[:, part].astype(F32) + c_ref[:, part].astype(F32)

    for h in range(heads):
        at = 3 * width * h
        queries = head_norm(total(at), q_gain_ref[h : h + 1, :])
        key_rows = jnp.concatenate([head_norm(total(at + width), k_gain_ref[h : h + 1, :]), spare], axis=0)
        value_rows = jnp.concatenate([total(at + 2 * width).astype(BF16), spare], axis=0)
        scores = lax.dot_general(
            queries, key_rows, (((1,), (1,)), ((), ())), preferred_element_type=F32
        ) / math.sqrt(width)
        scores = jnp.where(live, scores, -1e30)
        weights = jnp.exp(scores - jnp.max(scores, axis=-1, keepdims=True))
        weights = weights / jnp.sum(weights, axis=-1, keepdims=True)
        out_ref[:, width * h : width * (h + 1)] = jnp.dot(
            weights.astype(BF16), value_rows, preferred_element_type=F32
        ).astype(BF16)


def hidden_kernel(a_ref, b_ref, c_ref, bias_ref, attended_ref, out_ref):
    at = attended_ref.shape[1]
    out_ref[:, :at] = attended_ref[...]
    for k in range(0, a_ref.shape[1], 256):
        part = slice(k, k + 256)
        value = a_ref[:, part].astype(F32) + b_ref[:, part].astype(F32) + c_ref[:, part].astype(F32)
        value = value + bias_ref[:, part]
        value = 0.5 * value * (1.0 + lax.erf(value * math.sqrt(0.5)))
        out_ref[:, at + k : at + k + 256] = value.astype(BF16)


def out_kernel(crops, matrix_ref, *refs):
    out_refs = refs[-4:]
    pieces = list(refs[:-4])
    step = matrix_ref.shape[0] // 4

    def product(rows, at, size):
        for k, out_ref in enumerate(out_refs):
            out_ref[:, at : at + size] = lax.dot_general(
                matrix_ref[k * step : (k + 1) * step, :], rows, (((1,), (1,)), ((), ())), preferred_element_type=F32
            ).astype(BF16)

    at = 0
    for parts in crops:
        rows = [pieces.pop(0) for _ in range(parts)]
        if parts == 1:
            product(rows[0][:MAIN, :], at, MAIN)
        else:
            product(jnp.concatenate([rows[0][...], rows[1][: MAIN - rows[0].shape[0], :]], axis=0), at, MAIN)
        at += MAIN
    if pieces:
        product(pieces[0][...], at, pieces[0].shape[0])


def project_out(matrix, crops, rest=None):
    pieces = [p for crop in crops for p in crop] + ([rest] if rest is not None else [])
    length = MAIN * len(crops) + (rest.shape[0] if rest is not None else 0)
    width = matrix.shape[0]
    kernel = functools.partial(out_kernel, [len(crop) for crop in crops])
    return call(kernel, [(width // 4, length)] * 4, [matrix] + pieces)


def middle_kernel(*refs):
    term_refs, out_refs = refs[:-4], refs[-4:]
    step = out_refs[0].shape[0]
    at = 0
    for base in range(0, len(term_refs), 4):
        size = term_refs[base].shape[1]
        for k, out_ref in enumerate(out_refs):
            part = slice(k * step, (k + 1) * step)
            total = sum(ref[part, :].astype(F32) for ref in term_refs[base : base + 4])
            out_ref[:, at : at + size] = total.astype(BF16)
        at += size


def middle(groups):
    rows, length = groups[0][0].shape[0], sum(terms[0].shape[1] for terms in groups)
    return call(middle_kernel, [(rows // 4, length)] * 4, [term for terms in groups for term in terms])


def final_kernel(count, with_rest, *refs):
    terms, resid_refs, out_ref = refs[:4], refs[4:-1], refs[-1]

    def total(part):
        return terms[0][:, part].astype(F32) + terms[1][:, part].astype(F32) + terms[2][:, part].astype(F32) + terms[3][:, part].astype(F32)

    for k in range(count):
        part = slice(k * MAIN, (k + 1) * MAIN)
        out_ref[:, part] = (total(part) + resid_refs[k][:, :MAIN].astype(F32)).astype(BF16)
    if with_rest:
        part = slice(count * MAIN, count * MAIN + REST * len(resid_refs[count:]))
        rest = jnp.concatenate([ref[:, MAIN:].astype(F32) for ref in resid_refs[count:]], axis=1)
        out_ref[:, part] = (total(part) + rest).astype(BF16)


CHUNKS = ((0, 1, 2, 3, 6, 7), (4, 5))


def place_kernel(place_ref, *refs):
    out_ref, main_ref, rest_ref = refs[4:]
    count, thin, _ = out_ref.shape
    for d in range(2):
        parts = refs[2 * d : 2 * d + 2]
        for ref, blocks in zip(parts, CHUNKS):
            for k, r in enumerate(blocks):
                main_ref[count * d + r] = ref[:, k * MAIN : (k + 1) * MAIN].astype(F32)
        last = parts[1][:, len(CHUNKS[1]) * MAIN :].astype(F32)
        for r in range(count):
            rest_ref[count * d + r] = jnp.broadcast_to(last[:, REST * r : REST * r + 1], (thin, 128))
    for slot in range(count):
        at = place_ref[slot]
        out_ref[slot, :, :MAIN] = main_ref[at].astype(BF16)
        out_ref[slot, :, MAIN:] = rest_ref[at][:, :1].astype(BF16)


def shards(crops_in, crop_table, ln_gain, w_qkv, q_gain, k_gain, w_up, b_up, w_out, w_down):
    _, tokens, model_width = crops_in.shape
    count_y = lax.axis_size("my")
    count_x = lax.axis_size("mx")
    at_y = lax.axis_index("my")
    at_m = lax.axis_index("mx")
    at_d = lax.axis_index("dp")
    width = model_width // count_y
    thin = width // count_x
    heads_local, head_dim = w_out.shape[0], w_out.shape[1]
    split_at = heads_local * head_dim
    hidden_width = w_up.shape[1]

    place_y = at_y.astype(jnp.int32).reshape(1)
    crop = crops_in[0]
    last = jnp.pad(crop[MAIN:].astype(F32), ((0, 7), (0, 0)))
    place_x = (at_m // 4).astype(jnp.int32).reshape(1)
    barrier = lax.optimization_barrier

    (piece,) = pack(place_y, place_x, crop, last, width, FIRST)
    route = []
    for i in range(count_x):
        for j in range(count_y):
            route.append((i * count_y + j, i * count_y + (j ^ FIRST[i // 8])))
    piece = lax.ppermute(piece, ("mx", "my"), route)
    near_a, back_a, near_b, back_b, beside, mine = pack(place_y, place_x, crop, last, width, SECOND)
    piece, near_a, back_a, near_b, back_b = barrier((piece, near_a, back_a, near_b, back_b))
    near_a, back_a = swap(near_a, "my", 3), swap(back_a, "my", 7)
    near_b, back_b = swap(near_b, "my", 2), swap(back_b, "my", 6)
    pieces = sent([piece] * 4, 4)
    near_a, back_a, *pieces = barrier((near_a, back_a, *pieces))
    far_a, far_b = call(join_kernel, [(ROWS, width)] * 2, [place_x] + pieces, 1, 16_000_000)
    near_a, back_a, near_b, back_b, far_a, far_b = barrier((near_a, back_a, near_b, back_b, far_a, far_b))

    qkv_width = 3 * split_at
    weights_qkv = w_qkv.transpose(1, 2, 0, 3).reshape(3 * heads_local, width, head_dim)
    gain = ln_gain.astype(F32).reshape(1, width)
    resid = [None] * count_y
    place = at_m.astype(jnp.int32).reshape(1)

    def send(k, raw):
        other, resid[2 * k + 1] = call(
            send_kernel, [(ROWS, qkv_width + hidden_width), (thin, ROWS)], [place, raw, gain, weights_qkv, w_up], 1
        )
        return swap(other, "my", 1)

    def keep(k, raw, other):
        *terms, resid[2 * k] = call(
            keep_kernel,
            [(ROWS, qkv_width), (ROWS, hidden_width), (thin, ROWS)],
            [place, raw, gain, weights_qkv, w_up, other],
            1,
        )
        return terms

    def add(one, two):
        return call(add_kernel, [one.shape], [one, two])[0]

    far_other = send(2, far_a)
    far_parts = keep(2, far_b, far_other)
    far_qkv = swap(far_parts[0], "my", 2)
    far_up = swap(far_parts[1], "my", 6)
    beside, mine, _ = barrier((beside, mine, far_parts[0]))
    own_qkv, own_up = keep(0, mine, send(0, swap(beside, "my", 1)))
    near_other = send(1, near_a)
    back_other = send(3, back_a)
    near_qkv, near_up = keep(1, near_b, near_other)
    near_qkv = swap(near_qkv, "my", 2)
    back_qkv, back_up = keep(3, back_b, back_other)
    back_qkv = swap(add(back_qkv, far_qkv), "my", 6)
    near_up = add(near_up, far_up)
    near_up_sent, _ = barrier((near_up, near_qkv))
    near_up_got = swap(near_up_sent, "my", 2)
    back_up, _ = barrier((back_up, back_qkv))
    back_up = swap(back_up, "my", 6)

    w_out, w_down, _ = barrier((w_out, w_down, near_up))
    matrix = jnp.concatenate([w_out.reshape(split_at, width).T, w_down.T], axis=1).reshape(count_x, thin, -1)
    order = jnp.bitwise_xor(at_m, jnp.arange(count_x, dtype=jnp.int32))
    matrix = jnp.take(matrix, order, axis=0, mode="clip").reshape(width, -1)
    matrix, near_qkv = barrier((matrix, near_qkv))

    (attended,) = call(
        functools.partial(attend_kernel, tokens),
        [(ROWS, split_at)],
        [own_qkv, near_qkv, back_qkv, q_gain, k_gain],
    )
    (branch,) = call(
        hidden_kernel,
        [(ROWS, split_at + hidden_width)],
        [own_up, near_up_got, back_up, b_up.reshape(1, -1), attended],
    )

    cut = 128
    near_branch = swap(branch, "my", 2)
    back_branch = swap(branch, "my", 6)
    beside_branch = swap(branch, "my", 1)

    def spread(parts):
        return sent(parts, 4)

    def output(blocks, groups, rest):
        parts = middle(groups)
        parts = sent(parts, 1)
        base = [resid[r] for r in blocks] + (resid if rest else [])
        kernel = functools.partial(final_kernel, len(blocks), rest)
        (own,) = call(kernel, [parts[0].shape], list(parts) + base)
        return own, swap(own, "dp", 1)

    terms_0 = spread(project_out(matrix, [(branch,), (beside_branch,)]))
    near_branch, back_branch, *terms_0 = barrier((near_branch, back_branch, *terms_0))
    far_lead = swap(back_branch[:cut], "my", 2)
    far_trail = swap(near_branch[cut:], "my", 6)
    near_side = swap(near_branch, "my", 1)
    back_side = swap(back_branch, "my", 1)
    terms_1 = spread(project_out(matrix, [(near_branch,), (near_side,), (back_branch,), (back_side,)]))
    far_lead, far_trail, *terms_1 = barrier((far_lead, far_trail, *terms_1))
    own_0, other_0 = output(CHUNKS[0], [terms_0, terms_1], False)
    far_lead_side = swap(far_lead, "my", 1)
    far_trail_side = swap(far_trail, "my", 1)
    rest = jnp.concatenate(
        [
            piece[-REST:]
            for piece in (branch, beside_branch, near_branch, near_side, far_trail, far_trail_side, back_branch, back_side)
        ],
        axis=0,
    )
    parts = project_out(matrix, [(far_lead, far_trail), (far_lead_side, far_trail_side)], rest)
    terms = spread(parts)
    own_0, *terms = barrier((own_0, *terms))
    own_1, other_1 = output(CHUNKS[1], [terms], True)

    chosen = lax.dynamic_slice_in_dim(crop_table, at_d * count_y, count_y)
    place = jnp.bitwise_xor(chosen // count_y, at_d) * count_y + jnp.bitwise_xor(chosen % count_y, at_y)
    result = pl.pallas_call(
        place_kernel,
        out_shape=jax.ShapeDtypeStruct((count_y, thin, tokens), BF16),
        in_specs=[SMEM] + [pl.BlockSpec(memory_space=pltpu.VMEM)] * 4,
        out_specs=pl.BlockSpec(memory_space=pltpu.VMEM),
        scratch_shapes=[pltpu.VMEM((2 * count_y, thin, MAIN), F32), pltpu.VMEM((2 * count_y, thin, 128), F32)],
        compiler_params=pltpu.CompilerParams(vmem_limit_bytes=LIMIT),
        cost_estimate=pl.CostEstimate(flops=1000, bytes_accessed=1000, transcendentals=0),
    )(place.astype(jnp.int32), own_0, own_1, other_0, other_1)
    return result.transpose(0, 2, 1)


def solution(mesh):
    placed = (
        P(("dp", "my"), None, None),
        P(),
        P("my"),
        P("my", "mx", None, None),
        P("mx", None),
        P("mx", None),
        P("my", "mx"),
        P("mx"),
        P("mx", None, "my"),
        P("mx", "my"),
    )
    return jax.shard_map(
        shards, mesh=mesh, in_specs=placed, out_specs=P("dp", None, ("my", "mx")), check_vma=False
    )
```

```python
import functools
import math

import jax
import jax.numpy as jnp
from jax import lax
from jax.experimental import pallas as pl
from jax.experimental.pallas import tpu as pltpu
from jax.sharding import PartitionSpec as P

D = 6144
EPS = 1e-06
F32 = jnp.float32
BF16 = jnp.bfloat16
MAIN = 256
REST = 16
ROWS = MAIN + REST
LANES = 384
FIRST = (5, 4)
HALF = 144
SECOND = (3, 7, 2, 6, 1, 0)
LIMIT = 16 * 1024 * 1024
SMEM = pl.BlockSpec(memory_space=pltpu.SMEM)


def swap(value, axis, mask):
    count = lax.axis_size(axis)
    return lax.ppermute(value, axis, [(a, a ^ mask) for a in range(count)])


def call(kernel, outs, args, scalars=0):
    return pl.pallas_call(
        kernel,
        out_shape=[jax.ShapeDtypeStruct(shape, BF16) for shape in outs],
        in_specs=[SMEM] * scalars + [pl.BlockSpec(memory_space=pltpu.VMEM)] * (len(args) - scalars),
        out_specs=[pl.BlockSpec(memory_space=pltpu.VMEM)] * len(outs),
        compiler_params=pltpu.CompilerParams(vmem_limit_bytes=LIMIT),
        cost_estimate=pl.CostEstimate(flops=1000, bytes_accessed=1000, transcendentals=0),
    )(*args)


def row_statistics(piece_of, count):
    first = second = 0.0
    for k in range(count):
        piece = piece_of(k)
        first = first + jnp.sum(piece, axis=1, keepdims=True)
        second = second + jnp.sum(piece * piece, axis=1, keepdims=True)
    mean = first / D
    return mean, lax.rsqrt(second / D - mean * mean + EPS)


def split_table(mean, scale):
    rows = mean.shape[0]
    lane = lax.broadcasted_iota(jnp.int32, (rows, 128), 1)
    table = jnp.zeros((rows, 128), F32)
    for k, value in ((1, mean), (4, scale)):
        for part in range(3):
            high = value.astype(BF16).astype(F32)
            table = jnp.where(lane == k + part, high, table)
            value = value - high
    return table


def pack_kernel(count, masks, at_ref, x_ref, crop_ref, last_ref, *out_refs):
    width = crop_ref.shape[1] // count
    table = split_table(
        *row_statistics(lambda k: crop_ref[:MAIN, k * width : (k + 1) * width].astype(F32), count)
    )
    final = split_table(*row_statistics(lambda k: last_ref[:, k * width : (k + 1) * width], count))
    final = jnp.where(lax.broadcasted_iota(jnp.int32, final.shape, 0) == 0, final, 0.0)
    table = jnp.concatenate([table, final, jnp.zeros((LANES - MAIN - final.shape[0], 128), F32)], axis=0)
    stats = jnp.transpose(table)[:REST]
    stats = jnp.concatenate([stats, jnp.zeros((REST, width - LANES), F32)], axis=1)
    row = lax.broadcasted_iota(jnp.int32, (REST, width), 0)
    at_y = at_ref[0]
    if masks == FIRST:
        for k in range(4):

            @pl.when(x_ref[0] == k)
            def _(k=k):
                start = pl.multiple_of(jnp.bitwise_xor(at_y, masks[k // 2]) * width, width)
                columns = pl.ds(start, width)
                if k % 2 == 0:
                    out_refs[0][...] = crop_ref[:HALF, columns]
                else:
                    out_refs[0][: MAIN + HALF - ROWS, :] = crop_ref[ROWS - HALF : MAIN, columns]
                    final = jnp.where(row == 0, last_ref[:1, columns], stats)
                    out_refs[0][MAIN + HALF - ROWS :, :] = final.astype(BF16)

        return
    for out_ref, mask in zip(out_refs, masks):
        columns = pl.ds(pl.multiple_of(jnp.bitwise_xor(at_y, mask) * width, width), width)
        out_ref[:MAIN, :] = crop_ref[:MAIN, columns]
        out_ref[MAIN:, :] = jnp.where(row == 0, last_ref[:1, columns], stats).astype(BF16)


def pack(at_y, at_x, crop, last, width, masks):
    kernel = functools.partial(pack_kernel, crop.shape[1] // width, masks)
    shapes = [(HALF, width)] if masks == FIRST else [(ROWS, width)] * len(masks)
    return call(kernel, shapes, [at_y, at_x, crop, last], 2)


def join_kernel(x_ref, *refs):
    pieces, out_refs = refs[:4], refs[4:]
    for x in range(4):

        @pl.when(x_ref[0] == x)
        def _(x=x):
            for k, out_ref in enumerate(out_refs):
                out_ref[:HALF, :] = pieces[(2 * k) ^ x][...]
                out_ref[HALF:, :] = pieces[(2 * k + 1) ^ x][2 * HALF - ROWS :, :]


def normalised(raw_ref, gain_ref):
    stats = raw_ref[MAIN:ROWS, :LANES].astype(F32)
    mean = (stats[1:2] + stats[2:3]) + stats[3:4]
    scale = (stats[4:5] + stats[5:6]) + stats[6:7]
    row = lax.broadcasted_iota(jnp.int32, (128, LANES), 0)
    table = jnp.where(row == 0, mean, jnp.where(row == 1, scale, 0.0))
    table = jnp.transpose(table)[:ROWS]
    return ((raw_ref[:ROWS, :].astype(F32) - table[:, :1]) * table[:, 1:2] * gain_ref[...]).astype(BF16)


def thin_columns(at_ref, raw_ref, thin_ref):
    rows, width = thin_ref.shape[0], raw_ref.shape[1]
    row = lax.broadcasted_iota(jnp.int32, (rows, width), 0)
    column = lax.broadcasted_iota(jnp.int32, (rows, width), 1)
    chosen = jnp.where(column == row + at_ref[0] * rows, 1.0, 0.0).astype(BF16)
    thin_ref[...] = lax.dot_general(
        chosen, raw_ref[:ROWS, :], (((1,), (1,)), ((), ())), preferred_element_type=F32
    ).astype(BF16)


def products(normed, qkv_ref, up_ref):
    blocks, _, size = qkv_ref.shape
    for k in range(0, blocks, 3):
        matrix = jnp.concatenate([qkv_ref[k], qkv_ref[k + 1], qkv_ref[k + 2]], axis=1)
        yield k * size, jnp.dot(normed, matrix, preferred_element_type=F32)
    for k in range(0, up_ref.shape[1], 768):
        yield blocks * size + k, jnp.dot(normed, up_ref[:, k : k + 768], preferred_element_type=F32)


def send_kernel(at_ref, raw_ref, gain_ref, qkv_ref, up_ref, out_ref, thin_ref):
    for at, value in products(normalised(raw_ref, gain_ref), qkv_ref, up_ref):
        out_ref[:, at : at + value.shape[1]] = value.astype(BF16)
    thin_columns(at_ref, raw_ref, thin_ref)


def keep_kernel(at_ref, raw_ref, gain_ref, qkv_ref, up_ref, other_ref, *refs):
    out_refs, thin_ref = list(refs[:-1]), refs[-1]
    base = 0
    for at, value in products(normalised(raw_ref, gain_ref), qkv_ref, up_ref):
        size = value.shape[1]
        if at - base == out_refs[0].shape[1]:
            base += out_refs.pop(0).shape[1]
        value = value + other_ref[:, at : at + size].astype(F32)
        out_refs[0][:, at - base : at - base + size] = value.astype(BF16)
    thin_columns(at_ref, raw_ref, thin_ref)


def add_kernel(one_ref, two_ref, out_ref):
    out_ref[...] = (one_ref[...].astype(F32) + two_ref[...].astype(F32)).astype(BF16)


def head_norm(entries, gain_row):
    center = entries - jnp.mean(entries, axis=-1, keepdims=True)
    spread = jnp.mean(center * center, axis=-1, keepdims=True)
    return (center * lax.rsqrt(spread + EPS) * gain_row).astype(BF16)


def attend_kernel(tokens, a_ref, b_ref, c_ref, q_gain_ref, k_gain_ref, out_ref):
    heads, width = q_gain_ref.shape
    live = lax.broadcasted_iota(jnp.int32, (ROWS, LANES), 1) < tokens
    spare = jnp.zeros((LANES - ROWS, width), BF16)

    def total(at):
        part = slice(at, at + width)
        return a_ref[:, part].astype(F32) + b_ref[:, part].astype(F32) + c_ref[:, part].astype(F32)

    for h in range(heads):
        at = 3 * width * h
        queries = head_norm(total(at), q_gain_ref[h : h + 1, :])
        key_rows = jnp.concatenate([head_norm(total(at + width), k_gain_ref[h : h + 1, :]), spare], axis=0)
        value_rows = jnp.concatenate([total(at + 2 * width).astype(BF16), spare], axis=0)
        scores = lax.dot_general(
            queries, key_rows, (((1,), (1,)), ((), ())), preferred_element_type=F32
        ) / math.sqrt(width)
        scores = jnp.where(live, scores, -1e30)
        weights = jnp.exp(scores - jnp.max(scores, axis=-1, keepdims=True))
        weights = weights / jnp.sum(weights, axis=-1, keepdims=True)
        out_ref[:, width * h : width * (h + 1)] = jnp.dot(
            weights.astype(BF16), value_rows, preferred_element_type=F32
        ).astype(BF16)


def hidden_kernel(a_ref, b_ref, c_ref, bias_ref, attended_ref, out_ref):
    at = attended_ref.shape[1]
    out_ref[:, :at] = attended_ref[...]
    for k in range(0, a_ref.shape[1], 256):
        part = slice(k, k + 256)
        value = a_ref[:, part].astype(F32) + b_ref[:, part].astype(F32) + c_ref[:, part].astype(F32)
        value = value + bias_ref[:, part]
        value = 0.5 * value * (1.0 + lax.erf(value * math.sqrt(0.5)))
        out_ref[:, at + k : at + k + 256] = value.astype(BF16)


def out_kernel(crops, before, attn_ref, down_ref, *refs):
    out_refs = refs[-4:]
    pieces = list(refs[before:-4])
    step, split = attn_ref.shape[0] // 4, attn_ref.shape[1]
    dims = (((1,), (1,)), ((), ()))

    def product(rows, at, size):
        for k, out_ref in enumerate(out_refs):
            part = slice(k * step, (k + 1) * step)
            value = lax.dot_general(attn_ref[part, :], rows[:, :split], dims, preferred_element_type=F32)
            value = value + lax.dot_general(down_ref[part, :], rows[:, split:], dims, preferred_element_type=F32)
            out_ref[:, at : at + size] = value.astype(BF16)

    at = 0
    for ref, out_ref in zip(refs[:before], out_refs):
        at = ref.shape[1]
        out_ref[:, :at] = ref[...]
    for parts in crops:
        rows = [pieces.pop(0) for _ in range(parts)]
        if parts == 1:
            product(rows[0][:MAIN, :], at, MAIN)
        else:
            product(jnp.concatenate([rows[0][...], rows[1][: MAIN - rows[0].shape[0], :]], axis=0), at, MAIN)
        at += MAIN
    if pieces:
        product(pieces[0][...], at, pieces[0].shape[0])


def project_out(matrices, crops, rest=None, before=()):
    pieces = [p for crop in crops for p in crop] + ([rest] if rest is not None else [])
    length = MAIN * len(crops) + (rest.shape[0] if rest is not None else 0)
    width = matrices[0].shape[0]
    length += before[0].shape[1] if before else 0
    kernel = functools.partial(out_kernel, [len(crop) for crop in crops], len(before))
    return call(kernel, [(width // 4, length)] * 4, list(matrices) + list(before) + pieces)


def middle_kernel(*refs):
    term_refs, out_refs = refs[:-4], refs[-4:]
    step = out_refs[0].shape[0]
    at = 0
    for base in range(0, len(term_refs), 4):
        size = term_refs[base].shape[1]
        for k, out_ref in enumerate(out_refs):
            part = slice(k * step, (k + 1) * step)
            total = sum(ref[part, :].astype(F32) for ref in term_refs[base : base + 4])
            out_ref[:, at : at + size] = total.astype(BF16)
        at += size


def middle(groups):
    rows, length = groups[0][0].shape[0], sum(terms[0].shape[1] for terms in groups)
    return call(middle_kernel, [(rows // 4, length)] * 4, [term for terms in groups for term in terms])


def final_kernel(count, with_rest, *refs):
    terms, resid_refs, out_ref = refs[:4], refs[4:-1], refs[-1]

    def total(part):
        return terms[0][:, part].astype(F32) + terms[1][:, part].astype(F32) + terms[2][:, part].astype(F32) + terms[3][:, part].astype(F32)

    for k in range(count):
        part = slice(k * MAIN, (k + 1) * MAIN)
        out_ref[:, part] = (total(part) + resid_refs[k][:, :MAIN].astype(F32)).astype(BF16)
    if with_rest:
        part = slice(count * MAIN, count * MAIN + REST * len(resid_refs[count:]))
        rest = jnp.concatenate([ref[:, MAIN:].astype(F32) for ref in resid_refs[count:]], axis=1)
        out_ref[:, part] = (total(part) + rest).astype(BF16)


CHUNKS = ((0, 1, 2, 3), (6, 7, 4, 5))


def place_kernel(place_ref, *refs):
    out_ref, main_ref, rest_ref = refs[4:]
    count, thin, _ = out_ref.shape
    for d in range(2):
        parts = refs[2 * d : 2 * d + 2]
        for ref, blocks in zip(parts, CHUNKS):
            for k, r in enumerate(blocks):
                main_ref[count * d + r] = ref[:, k * MAIN : (k + 1) * MAIN].astype(F32)
        last = parts[1][:, len(CHUNKS[1]) * MAIN :].astype(F32)
        for r in range(count):
            rest_ref[count * d + r] = jnp.broadcast_to(last[:, REST * r : REST * r + 1], (thin, 128))
    for slot in range(count):
        at = place_ref[slot]
        out_ref[slot, :, :MAIN] = main_ref[at].astype(BF16)
        out_ref[slot, :, MAIN:] = rest_ref[at][:, :1].astype(BF16)


def shards(crops_in, crop_table, ln_gain, w_qkv, q_gain, k_gain, w_up, b_up, w_out, w_down):
    _, tokens, model_width = crops_in.shape
    count_y = lax.axis_size("my")
    count_x = lax.axis_size("mx")
    at_y = lax.axis_index("my")
    at_m = lax.axis_index("mx")
    at_d = lax.axis_index("dp")
    width = model_width // count_y
    thin = width // count_x
    heads_local, head_dim = w_out.shape[0], w_out.shape[1]
    split_at = heads_local * head_dim
    hidden_width = w_up.shape[1]

    place_y = at_y.astype(jnp.int32).reshape(1)
    crop = crops_in[0]
    last = jnp.pad(crop[MAIN:].astype(F32), ((0, 7), (0, 0)))
    place_x = (at_m // 4).astype(jnp.int32).reshape(1)
    barrier = lax.optimization_barrier

    (piece,) = pack(place_y, place_x, crop, last, width, FIRST)
    route = []
    for i in range(count_x):
        for j in range(count_y):
            route.append((i * count_y + j, i * count_y + (j ^ FIRST[i // 8])))
    piece = lax.ppermute(piece, ("mx", "my"), route)
    near_a, back_a, near_b, back_b, beside, mine = pack(place_y, place_x, crop, last, width, SECOND)
    near_a, back_a = barrier((swap(near_a, "my", 3), swap(back_a, "my", 7)))
    pieces = [piece] + [swap(piece, "mx", 4 * k) for k in (1, 2, 3)]
    near_b, back_b, _, _, _ = barrier((near_b, back_b, near_a, back_a, pieces[1]))
    near_b, back_b = swap(near_b, "my", 2), swap(back_b, "my", 6)
    near_a, back_a, near_b, back_b, *pieces = barrier((near_a, back_a, near_b, back_b, *pieces))
    far_a, far_b = call(join_kernel, [(ROWS, width)] * 2, [place_x] + pieces, 1)

    qkv_width = 3 * split_at
    weights_qkv = w_qkv.transpose(1, 2, 0, 3).reshape(3 * heads_local, width, head_dim)
    gain = ln_gain.astype(F32).reshape(1, width)
    resid = [None] * count_y
    place = at_m.astype(jnp.int32).reshape(1)

    def send(k, raw):
        other, resid[2 * k + 1] = call(
            send_kernel, [(ROWS, qkv_width + hidden_width), (thin, ROWS)], [place, raw, gain, weights_qkv, w_up], 1
        )
        return swap(other, "my", 1)

    def keep(k, raw, other):
        *terms, resid[2 * k] = call(
            keep_kernel,
            [(ROWS, qkv_width), (ROWS, hidden_width), (thin, ROWS)],
            [place, raw, gain, weights_qkv, w_up, other],
            1,
        )
        return terms

    def add(one, two):
        return call(add_kernel, [one.shape], [one, two])[0]

    far_other = send(2, far_a)
    far_parts = keep(2, far_b, far_other)
    far_qkv = swap(far_parts[0], "my", 2)
    far_up = swap(far_parts[1], "my", 6)
    beside, mine, _ = barrier((beside, mine, far_parts[0]))
    own_qkv, own_up = keep(0, mine, send(0, swap(beside, "my", 1)))
    near_other = send(1, near_a)
    back_other = send(3, back_a)
    near_qkv, near_up = keep(1, near_b, near_other)
    near_qkv = swap(near_qkv, "my", 2)
    back_qkv, back_up = keep(3, back_b, back_other)
    back_qkv = swap(add(back_qkv, far_qkv), "my", 6)
    near_up = add(near_up, far_up)
    near_up_sent, _ = barrier((near_up, near_qkv))
    near_up_got = swap(near_up_sent, "my", 2)
    back_up, _ = barrier((back_up, back_qkv))
    back_up = swap(back_up, "my", 6)

    w_out, w_down, _ = barrier((w_out, w_down, near_up))
    order = jnp.bitwise_xor(at_m, jnp.arange(count_x, dtype=jnp.int32))
    matrices = []
    for matrix in (w_out.reshape(split_at, width), w_down):
        matrix = jnp.take(matrix.T.reshape(count_x, thin, -1), order, axis=0, mode="clip")
        matrices.append(matrix.reshape(width, -1))
    *matrices, near_qkv = barrier((*matrices, near_qkv))

    (attended,) = call(
        functools.partial(attend_kernel, tokens),
        [(ROWS, split_at)],
        [own_qkv, near_qkv, back_qkv, q_gain, k_gain],
    )
    (branch,) = call(
        hidden_kernel,
        [(ROWS, split_at + hidden_width)],
        [own_up, near_up_got, back_up, b_up.reshape(1, -1), attended],
    )

    cut = 128
    near_branch = swap(branch, "my", 2)
    back_branch = swap(branch, "my", 6)
    beside_branch = swap(branch, "my", 1)

    def spread(parts):
        return [parts[0]] + [swap(parts[k], "mx", 4 * k) for k in (1, 2, 3)]

    def output(blocks, groups, rest):
        parts = middle(groups)
        parts = [parts[0]] + [swap(parts[k], "mx", k) for k in (1, 2, 3)]
        base = [resid[r] for r in blocks] + (resid if rest else [])
        kernel = functools.partial(final_kernel, len(blocks), rest)
        (own,) = call(kernel, [parts[0].shape], list(parts) + base)
        return own, swap(own, "dp", 1)

    terms_0 = spread(project_out(matrices, [(branch,), (beside_branch,)]))
    near_branch, back_branch, *terms_0 = barrier((near_branch, back_branch, *terms_0))
    far_lead = swap(back_branch[:cut], "my", 2)
    far_trail = swap(near_branch[cut:], "my", 6)
    near_side = swap(near_branch, "my", 1)
    back_side = swap(back_branch, "my", 1)
    terms_1 = spread(project_out(matrices, [(near_branch,), (near_side,)]))
    before = project_out(matrices, [(back_branch,), (back_side,)])
    far_lead, far_trail, *before = barrier((far_lead, far_trail, *before))
    far_lead, far_trail, *terms_1 = barrier((far_lead, far_trail, *terms_1))
    own_0, other_0 = output(CHUNKS[0], [terms_0, terms_1], False)
    far_lead_side = swap(far_lead, "my", 1)
    far_trail_side = swap(far_trail, "my", 1)
    rest = jnp.concatenate(
        [
            piece[-REST:]
            for piece in (branch, beside_branch, near_branch, near_side, far_trail, far_trail_side, back_branch, back_side)
        ],
        axis=0,
    )
    parts = project_out(matrices, [(far_lead, far_trail), (far_lead_side, far_trail_side)], rest, before)
    terms = spread(parts)
    own_0, *terms = barrier((own_0, *terms))
    own_1, other_1 = output(CHUNKS[1], [terms], True)

    chosen = lax.dynamic_slice_in_dim(crop_table, at_d * count_y, count_y)
    place = jnp.bitwise_xor(chosen // count_y, at_d) * count_y + jnp.bitwise_xor(chosen % count_y, at_y)
    result = pl.pallas_call(
        place_kernel,
        out_shape=jax.ShapeDtypeStruct((count_y, thin, tokens), BF16),
        in_specs=[SMEM] + [pl.BlockSpec(memory_space=pltpu.VMEM)] * 4,
        out_specs=pl.BlockSpec(memory_space=pltpu.VMEM),
        scratch_shapes=[pltpu.VMEM((2 * count_y, thin, MAIN), F32), pltpu.VMEM((2 * count_y, thin, 128), F32)],
        compiler_params=pltpu.CompilerParams(vmem_limit_bytes=LIMIT),
        cost_estimate=pl.CostEstimate(flops=1000, bytes_accessed=1000, transcendentals=0),
    )(place.astype(jnp.int32), own_0, own_1, other_0, other_1)
    return result.transpose(0, 2, 1)


def solution(mesh):
    placed = (
        P(("dp", "my"), None, None),
        P(),
        P("my"),
        P("my", "mx", None, None),
        P("mx", None),
        P("mx", None),
        P("my", "mx"),
        P("mx"),
        P("mx", None, "my"),
        P("mx", "my"),
    )
    return jax.shard_map(
        shards, mesh=mesh, in_specs=placed, out_specs=P("dp", None, ("my", "mx")), check_vma=False
    )
```

```python
import functools
import math

import jax
import jax.numpy as jnp
from jax import lax
from jax.experimental import pallas as pl
from jax.experimental.pallas import tpu as pltpu
from jax.sharding import PartitionSpec as P

D = 6144
EPS = 1e-06
F32 = jnp.float32
BF16 = jnp.bfloat16
MAIN = 256
REST = 16
ROWS = MAIN + REST
LANES = 384
FIRST = (5, 4)
HALF = 144
SECOND = (3, 7, 2, 6, 1, 0)
LIMIT = 16 * 1024 * 1024
SMEM = pl.BlockSpec(memory_space=pltpu.SMEM)


def swap(value, axis, mask):
    count = lax.axis_size(axis)
    return lax.ppermute(value, axis, [(a, a ^ mask) for a in range(count)])


def call(kernel, outs, args, scalars=0):
    return pl.pallas_call(
        kernel,
        out_shape=[jax.ShapeDtypeStruct(shape, BF16) for shape in outs],
        in_specs=[SMEM] * scalars + [pl.BlockSpec(memory_space=pltpu.VMEM)] * (len(args) - scalars),
        out_specs=[pl.BlockSpec(memory_space=pltpu.VMEM)] * len(outs),
        compiler_params=pltpu.CompilerParams(vmem_limit_bytes=LIMIT),
        cost_estimate=pl.CostEstimate(flops=1000, bytes_accessed=1000, transcendentals=0),
    )(*args)


def row_statistics(piece_of, count):
    first = second = 0.0
    for k in range(count):
        piece = piece_of(k)
        first = first + jnp.sum(piece, axis=1, keepdims=True)
        second = second + jnp.sum(piece * piece, axis=1, keepdims=True)
    mean = first / D
    return mean, lax.rsqrt(second / D - mean * mean + EPS)


def split_table(mean, scale):
    rows = mean.shape[0]
    lane = lax.broadcasted_iota(jnp.int32, (rows, 128), 1)
    table = jnp.zeros((rows, 128), F32)
    for k, value in ((1, mean), (4, scale)):
        for part in range(3):
            high = value.astype(BF16).astype(F32)
            table = jnp.where(lane == k + part, high, table)
            value = value - high
    return table


def pack_kernel(count, masks, at_ref, x_ref, crop_ref, last_ref, *out_refs):
    width = crop_ref.shape[1] // count
    table = split_table(
        *row_statistics(lambda k: crop_ref[:MAIN, k * width : (k + 1) * width].astype(F32), count)
    )
    final = split_table(*row_statistics(lambda k: last_ref[:, k * width : (k + 1) * width], count))
    final = jnp.where(lax.broadcasted_iota(jnp.int32, final.shape, 0) == 0, final, 0.0)
    table = jnp.concatenate([table, final, jnp.zeros((LANES - MAIN - final.shape[0], 128), F32)], axis=0)
    stats = jnp.transpose(table)[:REST]
    stats = jnp.concatenate([stats, jnp.zeros((REST, width - LANES), F32)], axis=1)
    row = lax.broadcasted_iota(jnp.int32, (REST, width), 0)
    at_y = at_ref[0]
    if masks == FIRST:
        for k in range(4):

            @pl.when(x_ref[0] == k)
            def _(k=k):
                start = pl.multiple_of(jnp.bitwise_xor(at_y, masks[k // 2]) * width, width)
                columns = pl.ds(start, width)
                if k % 2 == 0:
                    out_refs[0][...] = crop_ref[:HALF, columns]
                else:
                    out_refs[0][: MAIN + HALF - ROWS, :] = crop_ref[ROWS - HALF : MAIN, columns]
                    final = jnp.where(row == 0, last_ref[:1, columns], stats)
                    out_refs[0][MAIN + HALF - ROWS :, :] = final.astype(BF16)

        return
    for out_ref, mask in zip(out_refs, masks):
        columns = pl.ds(pl.multiple_of(jnp.bitwise_xor(at_y, mask) * width, width), width)
        out_ref[:MAIN, :] = crop_ref[:MAIN, columns]
        out_ref[MAIN:, :] = jnp.where(row == 0, last_ref[:1, columns], stats).astype(BF16)


def pack(at_y, at_x, crop, last, width, masks):
    kernel = functools.partial(pack_kernel, crop.shape[1] // width, masks)
    shapes = [(HALF, width)] if masks == FIRST else [(ROWS, width)] * len(masks)
    return call(kernel, shapes, [at_y, at_x, crop, last], 2)


def join_kernel(x_ref, *refs):
    pieces, out_refs = refs[:4], refs[4:]
    for x in range(4):

        @pl.when(x_ref[0] == x)
        def _(x=x):
            for k, out_ref in enumerate(out_refs):
                out_ref[:HALF, :] = pieces[(2 * k) ^ x][...]
                out_ref[HALF:, :] = pieces[(2 * k + 1) ^ x][2 * HALF - ROWS :, :]


def normalised(raw_ref, gain_ref):
    stats = raw_ref[MAIN:ROWS, :LANES].astype(F32)
    mean = (stats[1:2] + stats[2:3]) + stats[3:4]
    scale = (stats[4:5] + stats[5:6]) + stats[6:7]
    row = lax.broadcasted_iota(jnp.int32, (128, LANES), 0)
    table = jnp.where(row == 0, mean, jnp.where(row == 1, scale, 0.0))
    table = jnp.transpose(table)[:ROWS]
    return ((raw_ref[:ROWS, :].astype(F32) - table[:, :1]) * table[:, 1:2] * gain_ref[...]).astype(BF16)


def thin_columns(at_ref, raw_ref, thin_ref):
    rows, width = thin_ref.shape[0], raw_ref.shape[1]
    row = lax.broadcasted_iota(jnp.int32, (rows, width), 0)
    column = lax.broadcasted_iota(jnp.int32, (rows, width), 1)
    chosen = jnp.where(column == row + at_ref[0] * rows, 1.0, 0.0).astype(BF16)
    thin_ref[...] = lax.dot_general(
        chosen, raw_ref[:ROWS, :], (((1,), (1,)), ((), ())), preferred_element_type=F32
    ).astype(BF16)


def products(normed, qkv_ref, up_ref):
    blocks, _, size = qkv_ref.shape
    for k in range(0, blocks, 3):
        matrix = jnp.concatenate([qkv_ref[k], qkv_ref[k + 1], qkv_ref[k + 2]], axis=1)
        yield k * size, jnp.dot(normed, matrix, preferred_element_type=F32)
    for k in range(0, up_ref.shape[1], 768):
        yield blocks * size + k, jnp.dot(normed, up_ref[:, k : k + 768], preferred_element_type=F32)


def send_kernel(at_ref, raw_ref, gain_ref, qkv_ref, up_ref, out_ref, thin_ref):
    for at, value in products(normalised(raw_ref, gain_ref), qkv_ref, up_ref):
        out_ref[:, at : at + value.shape[1]] = value.astype(BF16)
    thin_columns(at_ref, raw_ref, thin_ref)


def keep_kernel(at_ref, raw_ref, gain_ref, qkv_ref, up_ref, other_ref, *refs):
    out_refs, thin_ref = list(refs[:-1]), refs[-1]
    base = 0
    for at, value in products(normalised(raw_ref, gain_ref), qkv_ref, up_ref):
        size = value.shape[1]
        if at - base == out_refs[0].shape[1]:
            base += out_refs.pop(0).shape[1]
        value = value + other_ref[:, at : at + size].astype(F32)
        out_refs[0][:, at - base : at - base + size] = value.astype(BF16)
    thin_columns(at_ref, raw_ref, thin_ref)


def add_kernel(one_ref, two_ref, out_ref):
    out_ref[...] = (one_ref[...].astype(F32) + two_ref[...].astype(F32)).astype(BF16)


def head_norm(entries, gain_row):
    center = entries - jnp.mean(entries, axis=-1, keepdims=True)
    spread = jnp.mean(center * center, axis=-1, keepdims=True)
    return (center * lax.rsqrt(spread + EPS) * gain_row).astype(BF16)


def attend_kernel(tokens, a_ref, b_ref, c_ref, q_gain_ref, k_gain_ref, out_ref):
    heads, width = q_gain_ref.shape
    live = lax.broadcasted_iota(jnp.int32, (ROWS, LANES), 1) < tokens
    spare = jnp.zeros((LANES - ROWS, width), BF16)

    def total(at):
        part = slice(at, at + width)
        return a_ref[:, part].astype(F32) + b_ref[:, part].astype(F32) + c_ref[:, part].astype(F32)

    for h in range(heads):
        at = 3 * width * h
        queries = head_norm(total(at), q_gain_ref[h : h + 1, :])
        key_rows = jnp.concatenate([head_norm(total(at + width), k_gain_ref[h : h + 1, :]), spare], axis=0)
        value_rows = jnp.concatenate([total(at + 2 * width).astype(BF16), spare], axis=0)
        scores = lax.dot_general(
            queries, key_rows, (((1,), (1,)), ((), ())), preferred_element_type=F32
        ) / math.sqrt(width)
        scores = jnp.where(live, scores, -1e30)
        weights = jnp.exp(scores - jnp.max(scores, axis=-1, keepdims=True))
        weights = weights / jnp.sum(weights, axis=-1, keepdims=True)
        out_ref[:, width * h : width * (h + 1)] = jnp.dot(
            weights.astype(BF16), value_rows, preferred_element_type=F32
        ).astype(BF16)


def hidden_kernel(a_ref, b_ref, c_ref, bias_ref, attended_ref, out_ref):
    at = attended_ref.shape[1]
    out_ref[:, :at] = attended_ref[...]
    for k in range(0, a_ref.shape[1], 256):
        part = slice(k, k + 256)
        value = a_ref[:, part].astype(F32) + b_ref[:, part].astype(F32) + c_ref[:, part].astype(F32)
        value = value + bias_ref[:, part]
        value = 0.5 * value * (1.0 + lax.erf(value * math.sqrt(0.5)))
        out_ref[:, at + k : at + k + 256] = value.astype(BF16)


def out_kernel(crops, before, attn_ref, down_ref, *refs):
    out_refs = refs[-4:]
    pieces = list(refs[before:-4])
    step, split = attn_ref.shape[0] // 4, attn_ref.shape[1]
    dims = (((1,), (1,)), ((), ()))

    def product(rows, at, size):
        for k, out_ref in enumerate(out_refs):
            part = slice(k * step, (k + 1) * step)
            value = lax.dot_general(attn_ref[part, :], rows[:, :split], dims, preferred_element_type=F32)
            value = value + lax.dot_general(down_ref[part, :], rows[:, split:], dims, preferred_element_type=F32)
            out_ref[:, at : at + size] = value.astype(BF16)

    at = 0
    for ref, out_ref in zip(refs[:before], out_refs):
        at = ref.shape[1]
        out_ref[:, :at] = ref[...]
    for parts in crops:
        rows = [pieces.pop(0) for _ in range(parts)]
        if parts == 1:
            product(rows[0][:MAIN, :], at, MAIN)
        else:
            product(jnp.concatenate([rows[0][...], rows[1][: MAIN - rows[0].shape[0], :]], axis=0), at, MAIN)
        at += MAIN
    if pieces:
        product(pieces[0][...], at, pieces[0].shape[0])


def project_out(matrices, crops, rest=None, before=()):
    pieces = [p for crop in crops for p in crop] + ([rest] if rest is not None else [])
    length = MAIN * len(crops) + (rest.shape[0] if rest is not None else 0)
    width = matrices[0].shape[0]
    length += before[0].shape[1] if before else 0
    kernel = functools.partial(out_kernel, [len(crop) for crop in crops], len(before))
    return call(kernel, [(width // 4, length)] * 4, list(matrices) + list(before) + pieces)


def middle_kernel(*refs):
    term_refs, out_refs = refs[:-4], refs[-4:]
    step = out_refs[0].shape[0]
    at = 0
    for base in range(0, len(term_refs), 4):
        size = term_refs[base].shape[1]
        for k, out_ref in enumerate(out_refs):
            part = slice(k * step, (k + 1) * step)
            total = sum(ref[part, :].astype(F32) for ref in term_refs[base : base + 4])
            out_ref[:, at : at + size] = total.astype(BF16)
        at += size


def middle(groups):
    rows, length = groups[0][0].shape[0], sum(terms[0].shape[1] for terms in groups)
    return call(middle_kernel, [(rows // 4, length)] * 4, [term for terms in groups for term in terms])


def final_kernel(count, with_rest, *refs):
    terms, resid_refs, out_ref = refs[:4], refs[4:-1], refs[-1]

    def total(part):
        return terms[0][:, part].astype(F32) + terms[1][:, part].astype(F32) + terms[2][:, part].astype(F32) + terms[3][:, part].astype(F32)

    for k in range(count):
        part = slice(k * MAIN, (k + 1) * MAIN)
        out_ref[:, part] = (total(part) + resid_refs[k][:, :MAIN].astype(F32)).astype(BF16)
    if with_rest:
        part = slice(count * MAIN, count * MAIN + REST * len(resid_refs[count:]))
        rest = jnp.concatenate([ref[:, MAIN:].astype(F32) for ref in resid_refs[count:]], axis=1)
        out_ref[:, part] = (total(part) + rest).astype(BF16)


CHUNKS = ((0, 1, 2, 3), (6, 7, 4, 5))


def place_kernel(place_ref, *refs):
    out_ref, main_ref, rest_ref = refs[4:]
    count, thin, _ = out_ref.shape
    for d in range(2):
        parts = refs[2 * d : 2 * d + 2]
        for ref, blocks in zip(parts, CHUNKS):
            for k, r in enumerate(blocks):
                main_ref[count * d + r] = ref[:, k * MAIN : (k + 1) * MAIN].astype(F32)
        last = parts[1][:, len(CHUNKS[1]) * MAIN :].astype(F32)
        for r in range(count):
            rest_ref[count * d + r] = jnp.broadcast_to(last[:, REST * r : REST * r + 1], (thin, 128))
    for slot in range(count):
        at = place_ref[slot]
        out_ref[slot, :, :MAIN] = main_ref[at].astype(BF16)
        out_ref[slot, :, MAIN:] = rest_ref[at][:, :1].astype(BF16)


def shards(crops_in, crop_table, ln_gain, w_qkv, q_gain, k_gain, w_up, b_up, w_out, w_down):
    _, tokens, model_width = crops_in.shape
    count_y = lax.axis_size("my")
    count_x = lax.axis_size("mx")
    at_y = lax.axis_index("my")
    at_m = lax.axis_index("mx")
    at_d = lax.axis_index("dp")
    width = model_width // count_y
    thin = width // count_x
    heads_local, head_dim = w_out.shape[0], w_out.shape[1]
    split_at = heads_local * head_dim
    hidden_width = w_up.shape[1]

    place_y = at_y.astype(jnp.int32).reshape(1)
    crop = crops_in[0]
    last = jnp.pad(crop[MAIN:].astype(F32), ((0, 7), (0, 0)))
    place_x = (at_m // 4).astype(jnp.int32).reshape(1)
    barrier = lax.optimization_barrier

    (piece,) = pack(place_y, place_x, crop, last, width, FIRST)
    route = []
    for i in range(count_x):
        for j in range(count_y):
            route.append((i * count_y + j, i * count_y + (j ^ FIRST[i // 8])))
    piece = lax.ppermute(piece, ("mx", "my"), route)
    near_a, back_a, near_b, back_b, beside, mine = pack(place_y, place_x, crop, last, width, SECOND)
    near_a, back_a = barrier((swap(near_a, "my", 3), swap(back_a, "my", 7)))
    pieces = [piece] + [swap(piece, "mx", 4 * k) for k in (1, 2, 3)]
    near_b, back_b, _, _, _ = barrier((near_b, back_b, near_a, back_a, pieces[2]))
    near_b, back_b = swap(near_b, "my", 2), swap(back_b, "my", 6)
    near_a, back_a, near_b, back_b, *pieces = barrier((near_a, back_a, near_b, back_b, *pieces))
    far_a, far_b = call(join_kernel, [(ROWS, width)] * 2, [place_x] + pieces, 1)

    qkv_width = 3 * split_at
    weights_qkv = w_qkv.transpose(1, 2, 0, 3).reshape(3 * heads_local, width, head_dim)
    gain = ln_gain.astype(F32).reshape(1, width)
    resid = [None] * count_y
    place = at_m.astype(jnp.int32).reshape(1)

    def send(k, raw):
        other, resid[2 * k + 1] = call(
            send_kernel, [(ROWS, qkv_width + hidden_width), (thin, ROWS)], [place, raw, gain, weights_qkv, w_up], 1
        )
        return swap(other, "my", 1)

    def keep(k, raw, other):
        *terms, resid[2 * k] = call(
            keep_kernel,
            [(ROWS, qkv_width), (ROWS, hidden_width), (thin, ROWS)],
            [place, raw, gain, weights_qkv, w_up, other],
            1,
        )
        return terms

    def add(one, two):
        return call(add_kernel, [one.shape], [one, two])[0]

    far_other = send(2, far_a)
    far_parts = keep(2, far_b, far_other)
    far_qkv = swap(far_parts[0], "my", 2)
    far_up = swap(far_parts[1], "my", 6)
    beside, mine, _ = barrier((beside, mine, far_parts[0]))
    own_qkv, own_up = keep(0, mine, send(0, swap(beside, "my", 1)))
    near_other = send(1, near_a)
    back_other = send(3, back_a)
    near_qkv, near_up = keep(1, near_b, near_other)
    near_qkv = swap(near_qkv, "my", 2)
    back_qkv, back_up = keep(3, back_b, back_other)
    back_qkv = swap(add(back_qkv, far_qkv), "my", 6)
    near_up = add(near_up, far_up)
    near_up_sent, _ = barrier((near_up, near_qkv))
    near_up_got = swap(near_up_sent, "my", 2)
    back_up, _ = barrier((back_up, back_qkv))
    back_up = swap(back_up, "my", 6)

    w_out, w_down, _ = barrier((w_out, w_down, near_up))
    order = jnp.bitwise_xor(at_m, jnp.arange(count_x, dtype=jnp.int32))
    matrices = []
    for matrix in (w_out.reshape(split_at, width), w_down):
        matrix = jnp.take(matrix.T.reshape(count_x, thin, -1), order, axis=0, mode="clip")
        matrices.append(matrix.reshape(width, -1))
    *matrices, near_qkv = barrier((*matrices, near_qkv))

    (attended,) = call(
        functools.partial(attend_kernel, tokens),
        [(ROWS, split_at)],
        [own_qkv, near_qkv, back_qkv, q_gain, k_gain],
    )
    (branch,) = call(
        hidden_kernel,
        [(ROWS, split_at + hidden_width)],
        [own_up, near_up_got, back_up, b_up.reshape(1, -1), attended],
    )

    cut = 128
    near_branch = swap(branch, "my", 2)
    back_branch = swap(branch, "my", 6)
    beside_branch = swap(branch, "my", 1)

    def spread(parts):
        return [parts[0]] + [swap(parts[k], "mx", 4 * k) for k in (1, 2, 3)]

    def output(blocks, groups, rest):
        parts = middle(groups)
        parts = [parts[0]] + [swap(parts[k], "mx", k) for k in (1, 3, 2)]
        base = [resid[r] for r in blocks] + (resid if rest else [])
        kernel = functools.partial(final_kernel, len(blocks), rest)
        (own,) = call(kernel, [parts[0].shape], list(parts) + base)
        return own, swap(own, "dp", 1)

    terms_0 = spread(project_out(matrices, [(branch,), (beside_branch,)]))
    near_branch, back_branch, *terms_0 = barrier((near_branch, back_branch, *terms_0))
    far_lead = swap(back_branch[:cut], "my", 2)
    far_trail = swap(near_branch[cut:], "my", 6)
    near_side = swap(near_branch, "my", 1)
    back_side = swap(back_branch, "my", 1)
    terms_1 = spread(project_out(matrices, [(near_branch,), (near_side,)]))
    before = project_out(matrices, [(back_branch,), (back_side,)])
    far_lead, far_trail, *before = barrier((far_lead, far_trail, *before))
    far_lead, far_trail, *terms_1 = barrier((far_lead, far_trail, *terms_1))
    own_0, other_0 = output(CHUNKS[0], [terms_0, terms_1], False)
    far_lead_side = swap(far_lead, "my", 1)
    far_trail_side = swap(far_trail, "my", 1)
    rest = jnp.concatenate(
        [
            piece[-REST:]
            for piece in (branch, beside_branch, near_branch, near_side, far_trail, far_trail_side, back_branch, back_side)
        ],
        axis=0,
    )
    parts = project_out(matrices, [(far_lead, far_trail), (far_lead_side, far_trail_side)], rest, before)
    terms = spread(parts)
    own_0, *terms = barrier((own_0, *terms))
    own_1, other_1 = output(CHUNKS[1], [terms], True)

    chosen = lax.dynamic_slice_in_dim(crop_table, at_d * count_y, count_y)
    place = jnp.bitwise_xor(chosen // count_y, at_d) * count_y + jnp.bitwise_xor(chosen % count_y, at_y)
    result = pl.pallas_call(
        place_kernel,
        out_shape=jax.ShapeDtypeStruct((count_y, thin, tokens), BF16),
        in_specs=[SMEM] + [pl.BlockSpec(memory_space=pltpu.VMEM)] * 4,
        out_specs=pl.BlockSpec(memory_space=pltpu.VMEM),
        scratch_shapes=[pltpu.VMEM((2 * count_y, thin, MAIN), F32), pltpu.VMEM((2 * count_y, thin, 128), F32)],
        compiler_params=pltpu.CompilerParams(vmem_limit_bytes=LIMIT),
        cost_estimate=pl.CostEstimate(flops=1000, bytes_accessed=1000, transcendentals=0),
    )(place.astype(jnp.int32), own_0, own_1, other_0, other_1)
    return result.transpose(0, 2, 1)


def solution(mesh):
    placed = (
        P(("dp", "my"), None, None),
        P(),
        P("my"),
        P("my", "mx", None, None),
        P("mx", None),
        P("mx", None),
        P("my", "mx"),
        P("mx"),
        P("mx", None, "my"),
        P("mx", "my"),
    )
    return jax.shard_map(
        shards, mesh=mesh, in_specs=placed, out_specs=P("dp", None, ("my", "mx")), check_vma=False
    )
```

```python
import functools
import math

import jax
import jax.numpy as jnp
from jax import lax
from jax.experimental import pallas as pl
from jax.experimental.pallas import tpu as pltpu
from jax.sharding import PartitionSpec as P

D = 6144
EPS = 1e-06
F32 = jnp.float32
BF16 = jnp.bfloat16
MAIN = 256
REST = 16
ROWS = MAIN + REST
LANES = 384
FIRST = (5, 4)
HALF = 144
SECOND = (3, 7, 2, 6, 1, 0)
LIMIT = 16 * 1024 * 1024
SMEM = pl.BlockSpec(memory_space=pltpu.SMEM)


def swap(value, axis, mask):
    count = lax.axis_size(axis)
    return lax.ppermute(value, axis, [(a, a ^ mask) for a in range(count)])


def call(kernel, outs, args, scalars=0):
    return pl.pallas_call(
        kernel,
        out_shape=[jax.ShapeDtypeStruct(shape, BF16) for shape in outs],
        in_specs=[SMEM] * scalars + [pl.BlockSpec(memory_space=pltpu.VMEM)] * (len(args) - scalars),
        out_specs=[pl.BlockSpec(memory_space=pltpu.VMEM)] * len(outs),
        compiler_params=pltpu.CompilerParams(vmem_limit_bytes=LIMIT),
        cost_estimate=pl.CostEstimate(flops=1000, bytes_accessed=1000, transcendentals=0),
    )(*args)


def row_statistics(piece_of, count):
    first = second = 0.0
    for k in range(count):
        piece = piece_of(k)
        first = first + jnp.sum(piece, axis=1, keepdims=True)
        second = second + jnp.sum(piece * piece, axis=1, keepdims=True)
    mean = first / D
    return mean, lax.rsqrt(second / D - mean * mean + EPS)


def split_table(mean, scale):
    rows = mean.shape[0]
    lane = lax.broadcasted_iota(jnp.int32, (rows, 128), 1)
    table = jnp.zeros((rows, 128), F32)
    for k, value in ((1, mean), (4, scale)):
        for part in range(3):
            high = value.astype(BF16).astype(F32)
            table = jnp.where(lane == k + part, high, table)
            value = value - high
    return table


def pack_kernel(count, masks, at_ref, x_ref, crop_ref, last_ref, *out_refs):
    width = crop_ref.shape[1] // count
    table = split_table(
        *row_statistics(lambda k: crop_ref[:MAIN, k * width : (k + 1) * width].astype(F32), count)
    )
    final = split_table(*row_statistics(lambda k: last_ref[:, k * width : (k + 1) * width], count))
    final = jnp.where(lax.broadcasted_iota(jnp.int32, final.shape, 0) == 0, final, 0.0)
    table = jnp.concatenate([table, final, jnp.zeros((LANES - MAIN - final.shape[0], 128), F32)], axis=0)
    stats = jnp.transpose(table)[:REST]
    stats = jnp.concatenate([stats, jnp.zeros((REST, width - LANES), F32)], axis=1)
    row = lax.broadcasted_iota(jnp.int32, (REST, width), 0)
    at_y = at_ref[0]
    if masks == FIRST:
        for k in range(4):

            @pl.when(x_ref[0] == k)
            def _(k=k):
                start = pl.multiple_of(jnp.bitwise_xor(at_y, masks[k // 2]) * width, width)
                columns = pl.ds(start, width)
                if k % 2 == 0:
                    out_refs[0][...] = crop_ref[:HALF, columns]
                else:
                    out_refs[0][: MAIN + HALF - ROWS, :] = crop_ref[ROWS - HALF : MAIN, columns]
                    final = jnp.where(row == 0, last_ref[:1, columns], stats)
                    out_refs[0][MAIN + HALF - ROWS :, :] = final.astype(BF16)

        return
    for out_ref, mask in zip(out_refs, masks):
        columns = pl.ds(pl.multiple_of(jnp.bitwise_xor(at_y, mask) * width, width), width)
        out_ref[:MAIN, :] = crop_ref[:MAIN, columns]
        out_ref[MAIN:, :] = jnp.where(row == 0, last_ref[:1, columns], stats).astype(BF16)


def pack(at_y, at_x, crop, last, width, masks):
    kernel = functools.partial(pack_kernel, crop.shape[1] // width, masks)
    shapes = [(HALF, width)] if masks == FIRST else [(ROWS, width)] * len(masks)
    return call(kernel, shapes, [at_y, at_x, crop, last], 2)


def join_kernel(x_ref, *refs):
    pieces, out_refs = refs[:4], refs[4:]
    for x in range(4):

        @pl.when(x_ref[0] == x)
        def _(x=x):
            for k, out_ref in enumerate(out_refs):
                out_ref[:HALF, :] = pieces[(2 * k) ^ x][...]
                out_ref[HALF:, :] = pieces[(2 * k + 1) ^ x][2 * HALF - ROWS :, :]


def normalised(raw_ref, gain_ref):
    stats = raw_ref[MAIN:ROWS, :LANES].astype(F32)
    mean = (stats[1:2] + stats[2:3]) + stats[3:4]
    scale = (stats[4:5] + stats[5:6]) + stats[6:7]
    row = lax.broadcasted_iota(jnp.int32, (128, LANES), 0)
    table = jnp.where(row == 0, mean, jnp.where(row == 1, scale, 0.0))
    table = jnp.transpose(table)[:ROWS]
    return ((raw_ref[:ROWS, :].astype(F32) - table[:, :1]) * table[:, 1:2] * gain_ref[...]).astype(BF16)


def thin_columns(at_ref, raw_ref, thin_ref):
    rows, width = thin_ref.shape[0], raw_ref.shape[1]
    row = lax.broadcasted_iota(jnp.int32, (rows, width), 0)
    column = lax.broadcasted_iota(jnp.int32, (rows, width), 1)
    chosen = jnp.where(column == row + at_ref[0] * rows, 1.0, 0.0).astype(BF16)
    thin_ref[...] = lax.dot_general(
        chosen, raw_ref[:ROWS, :], (((1,), (1,)), ((), ())), preferred_element_type=F32
    ).astype(BF16)


def products(normed, qkv_ref, up_ref):
    blocks, _, size = qkv_ref.shape
    for k in range(0, blocks, 3):
        matrix = jnp.concatenate([qkv_ref[k], qkv_ref[k + 1], qkv_ref[k + 2]], axis=1)
        yield k * size, jnp.dot(normed, matrix, preferred_element_type=F32)
    for k in range(0, up_ref.shape[1], 768):
        yield blocks * size + k, jnp.dot(normed, up_ref[:, k : k + 768], preferred_element_type=F32)


def send_kernel(at_ref, raw_ref, gain_ref, qkv_ref, up_ref, out_ref, thin_ref):
    for at, value in products(normalised(raw_ref, gain_ref), qkv_ref, up_ref):
        out_ref[:, at : at + value.shape[1]] = value.astype(BF16)
    thin_columns(at_ref, raw_ref, thin_ref)


def keep_kernel(at_ref, raw_ref, gain_ref, qkv_ref, up_ref, other_ref, *refs):
    out_refs, thin_ref = list(refs[:-1]), refs[-1]
    base = 0
    for at, value in products(normalised(raw_ref, gain_ref), qkv_ref, up_ref):
        size = value.shape[1]
        if at - base == out_refs[0].shape[1]:
            base += out_refs.pop(0).shape[1]
        value = value + other_ref[:, at : at + size].astype(F32)
        out_refs[0][:, at - base : at - base + size] = value.astype(BF16)
    thin_columns(at_ref, raw_ref, thin_ref)


def add_kernel(one_ref, two_ref, out_ref):
    out_ref[...] = (one_ref[...].astype(F32) + two_ref[...].astype(F32)).astype(BF16)


def head_norm(entries, gain_row):
    center = entries - jnp.mean(entries, axis=-1, keepdims=True)
    spread = jnp.mean(center * center, axis=-1, keepdims=True)
    return (center * lax.rsqrt(spread + EPS) * gain_row).astype(BF16)


def attend_kernel(tokens, a_ref, b_ref, c_ref, q_gain_ref, k_gain_ref, out_ref):
    heads, width = q_gain_ref.shape
    live = lax.broadcasted_iota(jnp.int32, (ROWS, LANES), 1) < tokens
    spare = jnp.zeros((LANES - ROWS, width), BF16)

    def total(at):
        part = slice(at, at + width)
        return a_ref[:, part].astype(F32) + b_ref[:, part].astype(F32) + c_ref[:, part].astype(F32)

    for h in range(heads):
        at = 3 * width * h
        queries = head_norm(total(at), q_gain_ref[h : h + 1, :])
        key_rows = jnp.concatenate([head_norm(total(at + width), k_gain_ref[h : h + 1, :]), spare], axis=0)
        value_rows = jnp.concatenate([total(at + 2 * width).astype(BF16), spare], axis=0)
        scores = lax.dot_general(
            queries, key_rows, (((1,), (1,)), ((), ())), preferred_element_type=F32
        ) / math.sqrt(width)
        scores = jnp.where(live, scores, -1e30)
        weights = jnp.exp(scores - jnp.max(scores, axis=-1, keepdims=True))
        weights = weights / jnp.sum(weights, axis=-1, keepdims=True)
        out_ref[:, width * h : width * (h + 1)] = jnp.dot(
            weights.astype(BF16), value_rows, preferred_element_type=F32
        ).astype(BF16)


def hidden_kernel(a_ref, b_ref, c_ref, bias_ref, attended_ref, out_ref):
    at = attended_ref.shape[1]
    out_ref[:, :at] = attended_ref[...]
    for k in range(0, a_ref.shape[1], 256):
        part = slice(k, k + 256)
        value = a_ref[:, part].astype(F32) + b_ref[:, part].astype(F32) + c_ref[:, part].astype(F32)
        value = value + bias_ref[:, part]
        value = 0.5 * value * (1.0 + lax.erf(value * math.sqrt(0.5)))
        out_ref[:, at + k : at + k + 256] = value.astype(BF16)


def out_kernel(crops, before, attn_ref, down_ref, *refs):
    out_refs = refs[-4:]
    pieces = list(refs[before:-4])
    step, split = attn_ref.shape[0] // 4, attn_ref.shape[1]
    dims = (((1,), (1,)), ((), ()))

    def product(rows, at, size):
        for k, out_ref in enumerate(out_refs):
            part = slice(k * step, (k + 1) * step)
            value = lax.dot_general(attn_ref[part, :], rows[:, :split], dims, preferred_element_type=F32)
            value = value + lax.dot_general(down_ref[part, :], rows[:, split:], dims, preferred_element_type=F32)
            out_ref[:, at : at + size] = value.astype(BF16)

    at = 0
    for ref, out_ref in zip(refs[:before], out_refs):
        at = ref.shape[1]
        out_ref[:, :at] = ref[...]
    for parts in crops:
        rows = [pieces.pop(0) for _ in range(parts)]
        if parts == 1:
            product(rows[0][:MAIN, :], at, MAIN)
        else:
            product(jnp.concatenate([rows[0][...], rows[1][: MAIN - rows[0].shape[0], :]], axis=0), at, MAIN)
        at += MAIN
    if pieces:
        product(pieces[0][...], at, pieces[0].shape[0])


def project_out(matrices, crops, rest=None, before=()):
    pieces = [p for crop in crops for p in crop] + ([rest] if rest is not None else [])
    length = MAIN * len(crops) + (rest.shape[0] if rest is not None else 0)
    width = matrices[0].shape[0]
    length += before[0].shape[1] if before else 0
    kernel = functools.partial(out_kernel, [len(crop) for crop in crops], len(before))
    return call(kernel, [(width // 4, length)] * 4, list(matrices) + list(before) + pieces)


def middle_kernel(*refs):
    term_refs, out_refs = refs[:-4], refs[-4:]
    step = out_refs[0].shape[0]
    at = 0
    for base in range(0, len(term_refs), 4):
        size = term_refs[base].shape[1]
        for k, out_ref in enumerate(out_refs):
            part = slice(k * step, (k + 1) * step)
            total = sum(ref[part, :].astype(F32) for ref in term_refs[base : base + 4])
            out_ref[:, at : at + size] = total.astype(BF16)
        at += size


def middle(groups):
    rows, length = groups[0][0].shape[0], sum(terms[0].shape[1] for terms in groups)
    return call(middle_kernel, [(rows // 4, length)] * 4, [term for terms in groups for term in terms])


def final_kernel(count, with_rest, *refs):
    terms, resid_refs, out_ref = refs[:4], refs[4:-1], refs[-1]

    def total(part):
        return terms[0][:, part].astype(F32) + terms[1][:, part].astype(F32) + terms[2][:, part].astype(F32) + terms[3][:, part].astype(F32)

    for k in range(count):
        part = slice(k * MAIN, (k + 1) * MAIN)
        out_ref[:, part] = (total(part) + resid_refs[k][:, :MAIN].astype(F32)).astype(BF16)
    if with_rest:
        part = slice(count * MAIN, count * MAIN + REST * len(resid_refs[count:]))
        rest = jnp.concatenate([ref[:, MAIN:].astype(F32) for ref in resid_refs[count:]], axis=1)
        out_ref[:, part] = (total(part) + rest).astype(BF16)


CHUNKS = ((0, 1, 2, 3), (6, 7, 4, 5))


def place_kernel(place_ref, *refs):
    out_ref, main_ref, rest_ref = refs[4:]
    count, thin, _ = out_ref.shape
    for d in range(2):
        parts = refs[2 * d : 2 * d + 2]
        for ref, blocks in zip(parts, CHUNKS):
            for k, r in enumerate(blocks):
                main_ref[count * d + r] = ref[:, k * MAIN : (k + 1) * MAIN].astype(F32)
        last = parts[1][:, len(CHUNKS[1]) * MAIN :].astype(F32)
        for r in range(count):
            rest_ref[count * d + r] = jnp.broadcast_to(last[:, REST * r : REST * r + 1], (thin, 128))
    for slot in range(count):
        at = place_ref[slot]
        out_ref[slot, :, :MAIN] = main_ref[at].astype(BF16)
        out_ref[slot, :, MAIN:] = rest_ref[at][:, :1].astype(BF16)


def shards(crops_in, crop_table, ln_gain, w_qkv, q_gain, k_gain, w_up, b_up, w_out, w_down):
    _, tokens, model_width = crops_in.shape
    count_y = lax.axis_size("my")
    count_x = lax.axis_size("mx")
    at_y = lax.axis_index("my")
    at_m = lax.axis_index("mx")
    at_d = lax.axis_index("dp")
    width = model_width // count_y
    thin = width // count_x
    heads_local, head_dim = w_out.shape[0], w_out.shape[1]
    split_at = heads_local * head_dim
    hidden_width = w_up.shape[1]

    place_y = at_y.astype(jnp.int32).reshape(1)
    crop = crops_in[0]
    last = jnp.pad(crop[MAIN:].astype(F32), ((0, 7), (0, 0)))
    place_x = (at_m // 4).astype(jnp.int32).reshape(1)
    barrier = lax.optimization_barrier

    (piece,) = pack(place_y, place_x, crop, last, width, FIRST)
    route = []
    for i in range(count_x):
        for j in range(count_y):
            route.append((i * count_y + j, i * count_y + (j ^ FIRST[i // 8])))
    piece = lax.ppermute(piece, ("mx", "my"), route)
    near_a, back_a, near_b, back_b, beside, mine = pack(place_y, place_x, crop, last, width, SECOND)
    near_a, back_a = barrier((swap(near_a, "my", 3), swap(back_a, "my", 7)))
    pieces = [piece] + [swap(piece, "mx", 4 * k) for k in (1, 2, 3)]
    near_b, back_b, _, _, _ = barrier((near_b, back_b, near_a, back_a, pieces[2]))
    near_b, back_b = swap(near_b, "my", 2), swap(back_b, "my", 6)
    near_a, back_a, near_b, back_b, *pieces = barrier((near_a, back_a, near_b, back_b, *pieces))
    far_a, far_b = call(join_kernel, [(ROWS, width)] * 2, [place_x] + pieces, 1)

    qkv_width = 3 * split_at
    weights_qkv = w_qkv.transpose(1, 2, 0, 3).reshape(3 * heads_local, width, head_dim)
    gain = ln_gain.astype(F32).reshape(1, width)
    resid = [None] * count_y
    place = at_m.astype(jnp.int32).reshape(1)

    def send(k, raw):
        other, resid[2 * k + 1] = call(
            send_kernel, [(ROWS, qkv_width + hidden_width), (thin, ROWS)], [place, raw, gain, weights_qkv, w_up], 1
        )
        return swap(other, "my", 1)

    def keep(k, raw, other):
        *terms, resid[2 * k] = call(
            keep_kernel,
            [(ROWS, qkv_width), (ROWS, hidden_width), (thin, ROWS)],
            [place, raw, gain, weights_qkv, w_up, other],
            1,
        )
        return terms

    def add(one, two):
        return call(add_kernel, [one.shape], [one, two])[0]

    far_other = send(2, far_a)
    far_parts = keep(2, far_b, far_other)
    far_qkv = swap(far_parts[0], "my", 2)
    far_up = swap(far_parts[1], "my", 6)
    beside, mine, _ = barrier((beside, mine, far_parts[0]))
    own_qkv, own_up = keep(0, mine, send(0, swap(beside, "my", 1)))
    near_other = send(1, near_a)
    back_other = send(3, back_a)
    near_qkv, near_up = keep(1, near_b, near_other)
    near_qkv = swap(near_qkv, "my", 2)
    back_qkv, back_up = keep(3, back_b, back_other)
    back_qkv = swap(add(back_qkv, far_qkv), "my", 6)
    near_up = add(near_up, far_up)
    near_up_sent, _ = barrier((near_up, near_qkv))
    near_up_got = swap(near_up_sent, "my", 2)
    back_up, _ = barrier((back_up, back_qkv))
    back_up = swap(back_up, "my", 6)

    w_out, w_down, _ = barrier((w_out, w_down, near_up))
    order = jnp.bitwise_xor(at_m, jnp.arange(count_x, dtype=jnp.int32))
    matrices = []
    for matrix in (w_out.reshape(split_at, width), w_down):
        matrix = jnp.take(matrix.T.reshape(count_x, thin, -1), order, axis=0, mode="clip")
        matrices.append(matrix.reshape(width, -1))
    *matrices, near_qkv = barrier((*matrices, near_qkv))

    (attended,) = call(
        functools.partial(attend_kernel, tokens),
        [(ROWS, split_at)],
        [own_qkv, near_qkv, back_qkv, q_gain, k_gain],
    )
    (branch,) = call(
        hidden_kernel,
        [(ROWS, split_at + hidden_width)],
        [own_up, near_up_got, back_up, b_up.reshape(1, -1), attended],
    )

    cut = 128
    near_branch = swap(branch, "my", 2)
    back_branch = swap(branch, "my", 6)
    beside_branch = swap(branch, "my", 1)

    def spread(parts):
        return [parts[0]] + [swap(parts[k], "mx", 4 * k) for k in (1, 3, 2)]

    def output(blocks, groups, rest):
        parts = middle(groups)
        parts = [parts[0]] + [swap(parts[k], "mx", k) for k in (1, 3, 2)]
        base = [resid[r] for r in blocks] + (resid if rest else [])
        kernel = functools.partial(final_kernel, len(blocks), rest)
        (own,) = call(kernel, [parts[0].shape], list(parts) + base)
        return own, swap(own, "dp", 1)

    terms_0 = spread(project_out(matrices, [(branch,), (beside_branch,)]))
    near_branch, back_branch, *terms_0 = barrier((near_branch, back_branch, *terms_0))
    far_lead = swap(back_branch[:cut], "my", 2)
    far_trail = swap(near_branch[cut:], "my", 6)
    near_side = swap(near_branch, "my", 1)
    back_side = swap(back_branch, "my", 1)
    terms_1 = spread(project_out(matrices, [(near_branch,), (near_side,)]))
    before = project_out(matrices, [(back_branch,), (back_side,)])
    far_lead, far_trail, *before = barrier((far_lead, far_trail, *before))
    far_lead, far_trail, *terms_1 = barrier((far_lead, far_trail, *terms_1))
    own_0, other_0 = output(CHUNKS[0], [terms_0, terms_1], False)
    far_lead_side = swap(far_lead, "my", 1)
    far_trail_side = swap(far_trail, "my", 1)
    rest = jnp.concatenate(
        [
            piece[-REST:]
            for piece in (branch, beside_branch, near_branch, near_side, far_trail, far_trail_side, back_branch, back_side)
        ],
        axis=0,
    )
    parts = project_out(matrices, [(far_lead, far_trail), (far_lead_side, far_trail_side)], rest, before)
    terms = spread(parts)
    own_0, *terms = barrier((own_0, *terms))
    own_1, other_1 = output(CHUNKS[1], [terms], True)

    chosen = lax.dynamic_slice_in_dim(crop_table, at_d * count_y, count_y)
    place = jnp.bitwise_xor(chosen // count_y, at_d) * count_y + jnp.bitwise_xor(chosen % count_y, at_y)
    result = pl.pallas_call(
        place_kernel,
        out_shape=jax.ShapeDtypeStruct((count_y, thin, tokens), BF16),
        in_specs=[SMEM] + [pl.BlockSpec(memory_space=pltpu.VMEM)] * 4,
        out_specs=pl.BlockSpec(memory_space=pltpu.VMEM),
        scratch_shapes=[pltpu.VMEM((2 * count_y, thin, MAIN), F32), pltpu.VMEM((2 * count_y, thin, 128), F32)],
        compiler_params=pltpu.CompilerParams(vmem_limit_bytes=LIMIT),
        cost_estimate=pl.CostEstimate(flops=1000, bytes_accessed=1000, transcendentals=0),
    )(place.astype(jnp.int32), own_0, own_1, other_0, other_1)
    return result.transpose(0, 2, 1)


def solution(mesh):
    placed = (
        P(("dp", "my"), None, None),
        P(),
        P("my"),
        P("my", "mx", None, None),
        P("mx", None),
        P("mx", None),
        P("my", "mx"),
        P("mx"),
        P("mx", None, "my"),
        P("mx", "my"),
    )
    return jax.shard_map(
        shards, mesh=mesh, in_specs=placed, out_specs=P("dp", None, ("my", "mx")), check_vma=False
    )
```
